512 devices in a mesh: member: 32 (over x, z_hi, y), mp: 16 (over z_lo, core).
Axes of the slice: x: 4, y: 4, z: 16 (z_hi: 2, z_lo: 8; z = z_hi * 8 + z_lo), core: 2. Of those that a mesh axis runs over, the one named last changes fastest.
Arguments:
- grid_fields: bfloat16 [32, 27648, 128], P('member', 'mp'), may hold values from -6 to 6
- edge_grid: int32 [2048, 32], P('mp'), may hold values from 0 to 27647, as said below
- edge_count: int32 [2048], P('mp'), may hold values from 16 to 32
- edge_weight: float32 [2048, 32], P('mp'), may hold values from 0.1 to 1
- enc_weight: bfloat16 [128, 1024], replicated, may hold values from -0.0625 to 0.0625
- qkv_weight: bfloat16 [3, 1024, 1024], P(None, 'mp')
- out_weight: bfloat16 [1024, 1024], P('mp'), may hold values from -0.75 to 0.75
- cotangent: bfloat16 [32, 2048, 1024], P('member', 'mp'), may hold values from -0.29882812 to 0.29882812
Outputs:
- layer_out: bfloat16 [32, 2048, 1024], P('member', 'mp')
- grad_qkv: float32 [3, 1024, 1024], P(None, 'mp')
- grad_out: float32 [1024, 1024], P('mp')
The draws below stay inside these ranges and needn't reach their ends.
Inputs may be any that keep to these rules, and one draw needn't show every extreme that they name: edge_grid[n, k] lies within 864 rows of the centre of node n's share of the grid, so its block of 1728 rows is n // 128 - 1, n // 128 or n // 128 + 1; slot 0 of the first node of each block of 128 nodes reaches the block before and slot 0 of its last node the block after, where those exist; slots at or after edge_count hold valid rows too.
All inputs are finite; a program needn't handle non-finite values.
Results may differ from the reference program's by a relative error of at most 0.03.
Values may be sent and summed in bfloat16 or wider, within the bound.
A program may use at most 128 MiB of HBM per device.

```python
import math
import jax
import jax.numpy as jnp
from jax import lax

D = 1024
HEADS = 16
C_IN = 128
K = 32
WINDOW = 512
NODE_DEV = 128
GRID_DEV = 1728
NODES = 2048
GRID = 27648
MEMBERS = 32


def draw_edge_grid(key, part):
    key = jax.random.fold_in(key, 11)
    node_ids = jnp.arange(NODES, dtype=jnp.int32)
    centre = (2 * node_ids + 1) * GRID // (2 * NODES)
    reach = GRID_DEV // 2
    offsets = jax.random.randint(key, (NODES, K), -reach, reach + 1, dtype=jnp.int32)
    slot_ids = jnp.arange(K, dtype=jnp.int32)[None, :]
    first_node = (node_ids % NODE_DEV == 0)[:, None]
    last_node = (node_ids % NODE_DEV == NODE_DEV - 1)[:, None]
    offsets = jnp.where(first_node & (slot_ids == 0), -reach, offsets)
    offsets = jnp.where(last_node & (slot_ids == 0), reach, offsets)
    return jnp.clip(centre[:, None] + offsets, 0, GRID - 1).astype(jnp.int32)


def draw_qkv_weight(key, part):
    key = jax.random.fold_in(key, 23)
    normal_draw = jax.random.normal(key, (3, D, D), jnp.float32) / math.sqrt(D)
    return normal_draw.astype(jnp.bfloat16)


def set_ends(drawn, rng, smallest, largest):
    longest = drawn.shape.index(max(drawn.shape))
    spots = []
    for shift in (0, 1):
        where = [jax.random.randint(jax.random.fold_in(rng, axis), (), 0, length) for axis, length in enumerate(drawn.shape)]
        where[longest] = (where[longest] + shift) % drawn.shape[longest]
        spots.append(tuple(where))
    return drawn.at[spots[0]].set(smallest).at[spots[1]].set(largest)


def levels(rng, extent, shards, low, high):
    def one(axis_at, shards_of):
        draws = jax.random.uniform(jax.random.fold_in(jax.random.fold_in(rng, 6), axis_at), (shards_of,), jnp.float32, low / len(shards), high / len(shards))
        return jnp.repeat(jnp.exp(draws), extent[axis_at] // shards_of).reshape((-1,) + (1,) * (len(extent) - axis_at - 1))

    gain = one(*shards[0])
    for cut in shards[1:]:
        gain = gain * one(*cut)
    return gain


def normal_values(own_key, extent, scale, most, pieces=(), held_as=jnp.bfloat16):
    entries = scale * jax.random.normal(own_key, extent, jnp.float32)
    if pieces:
        entries = entries * levels(own_key, extent, pieces, -0.22, 0.18)
    return jnp.clip(entries, -most, most).astype(held_as)


def setup_inputs(seed: int = 0) -> dict:
    splits = jax.random.split(jax.random.key(seed), 9)
    grid_fields = normal_values(splits[0], (MEMBERS, GRID, C_IN), 1.0, 6.0, ((0, 32), (1, 16)))
    edge_grid = draw_edge_grid(jax.random.fold_in(splits[8], 71), 0)
    edge_count = set_ends(jax.random.randint(splits[2], (NODES,), K // 2, K + 1), jax.random.fold_in(splits[2], 1), K // 2, K).astype(jnp.int32)
    edge_weight = jnp.clip(jnp.exp(math.log(1.0) - 2.3025851 * jax.random.uniform(splits[3], (NODES, K), jnp.float32) ** levels(splits[3], (NODES, K), ((0, 16),), -0.2, 0.2)), 0.1, 1.0)
    enc_weight = normal_values(splits[4], (C_IN, D), (C_IN * 64) ** -0.5, 0.0625)
    qkv_weight = draw_qkv_weight(jax.random.fold_in(splits[8], 71), 0)
    out_weight = normal_values(splits[6], (D, D), (D // 16) ** -0.5, 0.75, ((0, 16),))
    cotangent = normal_values(splits[7], (MEMBERS, NODES, D), 0.05, 0.29882812, ((0, 32), (1, 16)))
    return dict(grid_fields=grid_fields, edge_grid=edge_grid, edge_count=edge_count, edge_weight=edge_weight, enc_weight=enc_weight, qkv_weight=qkv_weight, out_weight=out_weight, cotangent=cotangent)


def layer_norm(hidden):
    centred = hidden - lax.optimization_barrier(jnp.mean(hidden, axis=-1, keepdims=True))
    spread = lax.optimization_barrier(jnp.mean(centred * centred, axis=-1, keepdims=True))
    return centred * lax.rsqrt(spread + 1e-05)

def window_attention(queries, key_rows, value_rows):
    length = queries.shape[0]
    head_count = queries.shape[1]
    head_width = queries.shape[2]
    block_rows = min(512, length)
    half_span = WINDOW // 2
    key_span = block_rows + 2 * half_span
    score_scale = 1.0 / head_width ** 0.5
    padding = jnp.zeros((half_span, head_count, head_width), queries.dtype)
    key_padded = jnp.concatenate([padding, key_rows, padding], axis=0)
    value_padded = jnp.concatenate([padding, value_rows, padding], axis=0)

    def one_block(block_start):
        query_block = lax.dynamic_slice_in_dim(queries, block_start, block_rows, 0)
        key_block = lax.dynamic_slice_in_dim(key_padded, block_start, key_span, 0)
        value_block = lax.dynamic_slice_in_dim(value_padded, block_start, key_span, 0)
        scores = jnp.einsum('ihe,jhe->hij', query_block, key_block, preferred_element_type=jnp.float32) * score_scale
        row_pos = block_start + jnp.arange(block_rows, dtype=jnp.int32)
        col_pos = block_start - half_span + jnp.arange(key_span, dtype=jnp.int32)
        inside = (col_pos[None, :] >= 0) & (col_pos[None, :] < length) & (jnp.abs(row_pos[:, None] - col_pos[None, :]) <= half_span)
        scores = jnp.where(inside[None], scores, -1e+30)
        row_max = lax.optimization_barrier(jnp.max(scores, axis=2, keepdims=True))
        weights = jnp.where(inside[None], jnp.exp(scores - row_max), 0.0)
        row_total = lax.optimization_barrier(jnp.sum(weights, axis=2, keepdims=True))
        probability = (weights / row_total).astype(jnp.bfloat16)
        return jnp.einsum('hij,jhe->ihe', probability, value_block, preferred_element_type=jnp.float32)
    block_starts = jnp.arange(length // block_rows, dtype=jnp.int32) * block_rows
    stacked = lax.map(one_block, block_starts)
    return stacked.reshape(length, head_count, head_width)

def encode(grid_rows, edge_grid, edge_count, edge_weight):
    slot_ids = jnp.arange(edge_grid.shape[1], dtype=jnp.int32)
    coeffs = jnp.where(slot_ids[None, :] < edge_count[:, None], edge_weight, 0.0)
    picked = jnp.take(grid_rows, edge_grid, axis=0).astype(jnp.float32)
    return lax.optimization_barrier(jnp.sum(coeffs[:, :, None] * picked, axis=1))

def reference(grid_fields, edge_grid, edge_count, edge_weight, enc_weight, qkv_weight, out_weight, cotangent):
    head_width = D // HEADS
    contract_cols = (((1,), (1,)), ((), ()))
    contract_rows = (((0,), (0,)), ((), ()))

    def member_pass(totals, inputs):
        grid_rows, cot_rows = inputs
        node_in = encode(grid_rows, edge_grid, edge_count, edge_weight).astype(jnp.bfloat16)
        hidden = jnp.dot(node_in, enc_weight, preferred_element_type=jnp.float32)
        normed = layer_norm(hidden).astype(jnp.bfloat16)
        projected = jnp.einsum('nd,cfd->cnf', normed, qkv_weight, preferred_element_type=jnp.float32).astype(jnp.bfloat16)
        shaped = projected.reshape(3, NODES, HEADS, head_width)
        attended_f, back_fn = jax.vjp(window_attention, shaped[0], shaped[1], shaped[2])
        attended = attended_f.astype(jnp.bfloat16).reshape(NODES, D)
        outputs = (hidden + jnp.dot(attended, out_weight, preferred_element_type=jnp.float32)).astype(jnp.bfloat16)
        d_attended = lax.dot_general(cot_rows, out_weight, contract_cols, preferred_element_type=jnp.float32).astype(jnp.bfloat16)
        cot_grads = back_fn(d_attended.reshape(NODES, HEADS, head_width).astype(jnp.float32))
        d_projected = jnp.stack(cot_grads).reshape(3, NODES, D)
        grad_qkv = jnp.einsum('cnf,nd->cfd', d_projected, normed, preferred_element_type=jnp.float32)
        grad_out = lax.dot_general(attended, cot_rows, contract_rows, preferred_element_type=jnp.float32)
        return ((totals[0] + grad_qkv, totals[1] + grad_out), outputs)
    initial = (jnp.zeros((3, D, D), jnp.float32), jnp.zeros((D, D), jnp.float32))
    (grad_qkv, grad_out), layer_out = lax.scan(member_pass, initial, (grid_fields, cotangent))
    return (layer_out, grad_qkv, grad_out)
```

```python
import functools
import math

import jax
import jax.numpy as jnp
from jax import lax
from jax.experimental import pallas as pl
from jax.experimental.pallas import tpu as pltpu
from jax.sharding import PartitionSpec as P

MESH = pl.DeviceIdType.MESH
BF16, F32 = jnp.bfloat16, jnp.float32
LOG2E = math.log2(math.e)

GRID_DEV = 1728
EXT = 41 * 128
BAND = 17 * 128
KEYS = 768
NT = (((1,), (1,)), ((), ()))
SHARD_AT = {0: 0, 4: 0, 7: 1, 3: 1, 1: 2, 5: 2, 2: 3, 6: 3}


def dot(a, b):
    return jnp.dot(a, b, preferred_element_type=F32)


def dot_nt(a, b):
    return lax.dot_general(a, b, NT, preferred_element_type=F32)


def attention_scratch():
    return dict(
        keys=pltpu.VMEM((1024, 256), BF16),
        keys_t=pltpu.VMEM((256, 1024), BF16),
        values=pltpu.VMEM((1024, 256), BF16),
        values_t=pltpu.VMEM((256, 1024), BF16),
        query=pltpu.VMEM((512, 256), BF16),
        query_tz=pltpu.VMEM((4, 128, 512), BF16),
        d_att_t=pltpu.VMEM((256, 512), BF16),
        bias=pltpu.VMEM((2, KEYS, 256), F32),
        weights=pltpu.VMEM((8, KEYS, 256), BF16),
        row_d=pltpu.VMEM((8, 1, 256), F32),
        d_att_z=pltpu.VMEM((8, 128, 256), BF16),
        att_t=pltpu.VMEM((256, 512), F32),
        d_query_t=pltpu.VMEM((256, 512), BF16),
        d_keys=pltpu.VMEM((1024, 256), F32),
        d_values=pltpu.VMEM((1024, 256), F32),
        left=pltpu.VMEM((256, 1024), BF16),
    )


def weight_grad(grads, c, left, right):
    def tile(t, carry):
        cols = pl.ds(pl.multiple_of(t * 256, 256), 256)
        product = dot(left(), right(cols)).astype(BF16)
        for j in range(4):
            grads[c, j, :, cols] = product[j * 64 : (j + 1) * 64]
        return carry

    lax.fori_loop(0, 4, tile, 0)


def attention(grp, normed, w, cot, grads, part, s, after_forward):
    key_pos = lax.broadcasted_iota(jnp.int32, (KEYS, 256), 0)
    query_pos = lax.broadcasted_iota(jnp.int32, (KEYS, 256), 1)
    for qb in range(2):
        node = key_pos + (grp * 512 - 256 + qb * 256)
        inside = (key_pos >= query_pos) & (key_pos <= query_pos + 512) & (node >= 0) & (node < 2048)
        s.bias[qb] = jnp.where(inside, 0.0, -1e30)
    s.d_keys[...] = jnp.zeros_like(s.d_keys)
    s.d_values[...] = jnp.zeros_like(s.d_values)

    wq = w[:, 0].reshape(256, 1024)
    wk = w[:, 1].reshape(256, 1024)
    wv = w[:, 2].reshape(256, 1024)
    wo = w[:, 3].reshape(256, 1024)

    def project(t, carry):
        rows = pl.ds(pl.multiple_of(t * 256, 256), 256)
        block = normed[rows, :]
        s.keys[rows, :] = dot_nt(block, wk).astype(BF16)
        s.values[rows, :] = dot_nt(block, wv).astype(BF16)
        s.keys_t[:, rows] = dot_nt(wk, block).astype(BF16)
        s.values_t[:, rows] = dot_nt(wv, block).astype(BF16)
        return carry

    lax.fori_loop(0, 4, project, 0)

    def project_own(t, carry):
        rows = pl.ds(pl.multiple_of(t * 256, 256), 256)
        block = normed[pl.ds(pl.multiple_of(t * 256 + 256, 256), 256), :]
        s.query[rows, :] = (dot_nt(block, wq) * (LOG2E / 8)).astype(BF16)
        query_t = dot_nt(wq, block) * (LOG2E / 8)
        upper = lax.broadcasted_iota(jnp.int32, (128, 256), 0) < 64
        for h in range(4):
            pair = query_t[h // 2 * 128 : h // 2 * 128 + 128]
            keep = upper if h % 2 == 0 else ~upper
            s.query_tz[h, :, rows] = jnp.where(keep, pair, 0.0).astype(BF16)
        cot_rows = cot[pl.ds(t * 2, 2)].reshape(256, 1024)
        s.d_att_t[:, rows] = dot_nt(wo, cot_rows).astype(BF16)
        return carry

    lax.fori_loop(0, 2, project_own, 0)

    def place(i):
        pair, qb = lax.div(i, 2), lax.rem(i, 2)
        key_rows = pl.ds(pl.multiple_of(qb * 256, 256), KEYS)
        lanes = pl.ds(pl.multiple_of(pair * 128, 128), 128)
        cols = pl.ds(pl.multiple_of(qb * 256, 256), 256)
        return pair, qb, key_rows, lanes, cols

    def head_rows(pair, hh):
        return pl.ds(pl.multiple_of(pair * 128 + hh * 64, 64), 64)

    def forward(i, carry):
        pair, qb, key_rows, lanes, cols = place(i)
        key_block = s.keys[key_rows, lanes]
        all_weights, scaled = [], []
        for hh in range(2):
            scores = dot(key_block, s.query_tz[pair * 2 + hh, :, cols]) + s.bias[qb]
            weight = jnp.exp2(scores - jnp.max(scores, axis=0, keepdims=True))
            inverse = 1.0 / jnp.sum(weight, axis=0, keepdims=True)
            weight = weight.astype(BF16)
            s.weights[i * 2 + hh] = weight
            all_weights.append(weight)
            rows = head_rows(pair, hh)
            out = dot(s.values_t[rows, key_rows], weight) * inverse
            d_out = s.d_att_t[rows, cols].astype(F32)
            s.row_d[i * 2 + hh] = jnp.sum(d_out * out, axis=0, keepdims=True) * inverse
            s.att_t[rows, cols] = out
            scaled.append(d_out * inverse)
        both = jnp.concatenate(scaled, axis=0)
        upper = lax.broadcasted_iota(jnp.int32, (128, 256), 0) < 64
        s.d_att_z[i * 2] = jnp.where(upper, both, 0.0).astype(BF16)
        s.d_att_z[i * 2 + 1] = jnp.where(upper, 0.0, both).astype(BF16)
        rows_form = both.T
        low = lax.broadcasted_iota(jnp.int32, (256, 128), 1) < 64
        s.d_values[key_rows, lanes] += dot(
            all_weights[0], jnp.where(low, rows_form, 0.0).astype(BF16)
        ) + dot(all_weights[1], jnp.where(low, 0.0, rows_form).astype(BF16))
        return carry

    lax.fori_loop(0, 4, forward, 0)

    def project_out(t, carry):
        rows = pl.ds(pl.multiple_of(t * 128, 128), 128)
        attended = s.att_t[:, rows].T.astype(BF16)
        part[t] = dot(attended, wo).astype(BF16)
        return carry

    lax.fori_loop(0, 4, project_out, 0)
    s.left[:, 0:512] = s.att_t[...].astype(BF16)
    weight_grad(
        grads, 3, lambda: s.left[:, 0:512], lambda cols: cot[:, :, cols].reshape(512, 256)
    )
    s.left[...] = s.d_values[...].T.astype(BF16)
    weight_grad(grads, 2, lambda: s.left[...], lambda cols: normed[:, cols])
    after_forward()

    def backward(i, carry):
        pair, qb, key_rows, lanes, cols = place(i)
        value_block = s.values[key_rows, lanes]
        low = lax.broadcasted_iota(jnp.int32, (256, 128), 1) < 64
        query = s.query[cols, lanes]
        d_keys = jnp.zeros((KEYS, 128), F32)
        for hh in range(2):
            d_weight = dot(value_block, s.d_att_z[i * 2 + hh])
            d_scores = (s.weights[i * 2 + hh].astype(F32) * (d_weight - s.row_d[i * 2 + hh])).astype(BF16)
            rows = head_rows(pair, hh)
            s.d_query_t[rows, cols] = (dot(s.keys_t[rows, key_rows], d_scores) * 0.125).astype(BF16)
            d_keys += dot(d_scores, jnp.where(low if hh == 0 else ~low, query, jnp.zeros_like(query)))
        s.d_keys[key_rows, lanes] += d_keys * (1.0 / LOG2E)
        return carry

    lax.fori_loop(0, 4, backward, 0)
    weight_grad(grads, 0, lambda: s.d_query_t[...], lambda cols: normed[256:768, cols])
    s.left[...] = s.d_keys[...].T.astype(BF16)
    weight_grad(grads, 1, lambda: s.left[...], lambda cols: normed[:, cols])


class Names:
    def __init__(self, names, refs):
        self.__dict__.update(zip(names, refs, strict=True))


def exchange_scratch():
    return dict(
        ext=pltpu.VMEM((EXT, 128), BF16),
        place=pltpu.VMEM((128, EXT), BF16),
        coef=pltpu.VMEM((128, 32), F32),
        nodes=pltpu.VMEM((8, 128, 128), BF16),
        normed=pltpu.VMEM((1024, 1024), BF16),
        w=pltpu.VMEM((4, 4, 64, 1024), BF16),
        cot=pltpu.VMEM((4, 128, 1024), BF16),
        grads=pltpu.VMEM((4, 4, 64, 1024), BF16),
        part=pltpu.VMEM((4, 128, 1024), BF16),
        part_in=pltpu.VMEM((3, 128, 1024), BF16),
        in_a1=pltpu.VMEM((4, 3, 4, 16, 512), BF16),
        in_b1=pltpu.VMEM((4, 3, 4, 16, 512), BF16),
        sum_a1=pltpu.VMEM((4, 4, 16, 512), BF16),
        sum_b1=pltpu.VMEM((4, 4, 16, 512), BF16),
        in_a2=pltpu.VMEM((4, 3, 4, 16, 128), BF16),
        in_b2=pltpu.VMEM((4, 3, 4, 16, 128), BF16),
        plane=pltpu.VMEM((4, 4, 2, 16, 128), BF16),
        in_z=pltpu.VMEM((7, 2, 2, 16, 128), BF16),
        total=pltpu.VMEM((4, 2, 16, 128), BF16),
        gathered=pltpu.VMEM((4, 64, 1024), BF16),
    )


EXCHANGE = exchange_scratch()
ATTENTION = attention_scratch()
SEMS = 128


def step_kernel(*refs):
    inputs = Names(("grid", "edge", "count", "edge_w", "enc", "wqkv", "wo", "cot"), refs[:8])
    layer_out, grad_qkv, grad_out = refs[8:11]
    b = Names(tuple(EXCHANGE), refs[11 : 11 + len(EXCHANGE)])
    s = Names(tuple(ATTENTION), refs[11 + len(EXCHANGE) : 11 + len(EXCHANGE) + len(ATTENTION)])
    send_sem, recv_sem, local_sem = refs[11 + len(EXCHANGE) + len(ATTENTION) :]

    member, mp = lax.axis_index("member"), lax.axis_index("mp")
    x, hi, y = lax.div(member, 8), lax.rem(lax.div(member, 4), 2), lax.rem(member, 4)
    g = hi * 16 + mp
    r, grp = lax.rem(mp, 4), lax.div(mp, 4)

    def at_col(place):
        there = lax.rem(place + 32, 32)
        return (x * 8 + lax.div(there, 16) * 4 + y, lax.rem(there, 16))

    def at_x(d):
        return (lax.rem(x + d, 4) * 8 + hi * 4 + y, mp)

    def at_y(d):
        return (x * 8 + hi * 4 + lax.rem(y + d, 4), mp)

    def mate(d):
        return at_col(g - r + lax.rem(r + d, 4))

    started, used = [], [0]

    def take(n=1):
        used[0] += n
        return used[0] - n

    def push(src, dst, recv, device):
        copy = pltpu.make_async_remote_copy(
            src_ref=src,
            dst_ref=dst,
            send_sem=send_sem.at[len(started)],
            recv_sem=recv_sem.at[recv],
            device_id=device,
            device_id_type=MESH,
        )
        copy.start()
        started.append(copy)

    def arrived(dst, recv):
        pltpu.make_async_copy(dst, dst, recv_sem.at[recv]).wait()

    def tile16(k):
        return pl.ds(pl.multiple_of(k * 16, 16), 16)

    def tile128(k):
        return pl.ds(pl.multiple_of(k * 128, 128), 128)

    LOW, HIGH = pl.ds(0, 512), pl.ds(512, 512)

    barrier = pltpu.get_barrier_semaphore()
    sources = [at_col(g + 4 * d) for d in range(1, 8)]
    sources += [at_x(d) for d in range(1, 4)] + [at_y(d) for d in range(1, 4)]
    sources += [mate(d) for d in range(1, 4)]
    sources += [at_col(g - r + d) for d in (-2, -1, 4, 5)]
    for device in sources:
        pl.semaphore_signal(barrier, inc=1, device_id=device, device_id_type=MESH)
    own_grid = pltpu.make_async_copy(inputs.grid, b.ext.at[pl.ds(GRID_DEV, GRID_DEV)], local_sem.at[0])
    own_w = pltpu.make_async_copy(inputs.wqkv, b.w.at[0, pl.ds(0, 3)], local_sem.at[1])
    own_wo = pltpu.make_async_copy(inputs.wo, b.w.at[0, 3], local_sem.at[2])
    own_cot = pltpu.make_async_copy(inputs.cot, b.cot.at[r], local_sem.at[3])
    for copy in (own_grid, own_w, own_wo, own_cot):
        copy.start()
    pl.semaphore_wait(barrier, len(sources))

    left_rows, right_rows = pl.ds(0, GRID_DEV), pl.ds(2 * GRID_DEV, GRID_DEV)
    grid_sem = take(2)
    push(inputs.grid, b.ext.at[left_rows], grid_sem, at_col(g + 1))
    push(inputs.grid, b.ext.at[right_rows], grid_sem + 1, at_col(g - 1))

    own_w.wait()
    own_wo.wait()
    piece_a = (tile16(y), tile128(x))
    piece_b = (tile16(x), tile128(y + 4))
    ALL = slice(None)
    z_sem = take(6)
    for n, (j, off) in enumerate(((1, 4), (2, -4), (3, 8))):
        push(b.w.at[(0, ALL) + piece_a], b.w.at[(j, ALL) + piece_a], z_sem + n, at_col(g + off))
        push(b.w.at[(0, ALL) + piece_b], b.w.at[(j, ALL) + piece_b], z_sem + 3 + n, at_col(g + off))

    b.place[...] = jnp.zeros_like(b.place)
    b.ext[pl.ds(3 * GRID_DEV, EXT - 3 * GRID_DEV), :] = jnp.zeros((EXT - 3 * GRID_DEV, 128), BF16)
    counts = jnp.broadcast_to(inputs.count[...].astype(F32), (128, 128)).T[:, :32]
    slot = lax.broadcasted_iota(jnp.int32, (128, 32), 1).astype(F32)
    b.coef[...] = jnp.where(slot < counts, inputs.edge_w[...], 0.0)

    def build(k, carry):
        rows = tile16(k)
        start = pl.multiple_of(lax.div(862 + 216 * k, 128) * 128, 128)
        index = inputs.edge[rows, :] - ((mp - 1) * GRID_DEV + start)
        coef = b.coef[rows, :]
        lane = lax.broadcasted_iota(jnp.int32, (16, BAND), 1)
        total = jnp.zeros((16, BAND), F32)
        for e in range(32):
            total += jnp.where(lane == index[:, e : e + 1], coef[:, e : e + 1], 0.0)
        b.place[rows, pl.ds(start, BAND)] = total.astype(BF16)
        return carry

    lax.fori_loop(0, 8, build, 0)

    others = pl.ds(1, 3)
    w_all = b.w.at[others]
    for n in range(3):
        arrived(b.w.at[(n + 1, ALL) + piece_a], z_sem + n)
        arrived(b.w.at[(n + 1, ALL) + piece_b], z_sem + 3 + n)
    first_a, first_b = take(3), take(3)
    for d in range(1, 4):
        part_a = b.w.at[(others, ALL) + piece_a]
        part_b = b.w.at[(others, ALL) + piece_b]
        push(part_a, part_a, first_a + d - 1, at_x(d))
        push(part_b, part_b, first_b + d - 1, at_y(d))

    own_grid.wait()
    arrived(b.ext.at[left_rows], grid_sem)
    arrived(b.ext.at[right_rows], grid_sem + 1)
    node_in = dot(b.place[...], b.ext[...]).astype(BF16)
    b.nodes[pl.ds(r + 2, 1)] = node_in[None]
    mine = b.nodes.at[r + 2]
    mate_sem, next_sem = take(3), take(4)
    for d in range(1, 4):
        push(mine, mine, mate_sem + d - 1, mate(d))
    near = jnp.where(r < 2, g - r - 4, g - r + 4)
    for t in range(4):
        push(mine, b.nodes.at[lax.rem(r + 6, 8)], next_sem + r, at_col(near + t))
    own_cot.wait()
    cot_sem = take(3)
    for d in range(1, 4):
        push(b.cot.at[r], b.cot.at[r], cot_sem + d - 1, mate(d))

    second_a, second_b = take(3), take(3)
    for d in range(1, 4):
        arrived(b.w.at[(others, ALL) + piece_a], first_a + d - 1)
        arrived(b.w.at[(others, ALL) + piece_b], first_b + d - 1)
    row_a = (tile16(y), LOW)
    row_b = (tile16(x), HIGH)
    for d in range(1, 4):
        part_a = b.w.at[(others, ALL) + row_a]
        part_b = b.w.at[(others, ALL) + row_b]
        push(part_a, part_a, second_a + d - 1, at_y(d))
        push(part_b, part_b, second_b + d - 1, at_x(d))

    for d in range(1, 4):
        arrived(mine, mate_sem + d - 1)
    for t, place in enumerate((6, 7, 0, 1)):
        arrived(b.nodes.at[place], next_sem + t)

    def normalise(k, carry):
        hidden = dot(b.nodes[k], inputs.enc[...])
        centred = hidden - jnp.mean(hidden, axis=1, keepdims=True)
        spread = jnp.mean(centred * centred, axis=1, keepdims=True)
        b.normed[tile128(k), :] = (centred * lax.rsqrt(spread + 1e-05)).astype(BF16)
        return carry

    lax.fori_loop(0, 8, normalise, 0)

    for d in range(1, 4):
        arrived(b.w.at[(others, ALL) + row_a], second_a + d - 1)
        arrived(b.w.at[(others, ALL) + row_b], second_b + d - 1)
        arrived(b.cot.at[r], cot_sem + d - 1)

    sems_1 = [take(6) for _ in range(4)]
    sems_2 = [take(6) for _ in range(4)]

    def plane_first(c):
        for d in range(1, 4):
            to_y, to_x = lax.rem(y + d, 4), lax.rem(x + d, 4)
            push(b.grads.at[c, :, tile16(to_y), LOW], b.in_a1.at[c, d - 1], sems_1[c] + d - 1, at_y(d))
            push(b.grads.at[c, :, tile16(to_x), HIGH], b.in_b1.at[c, d - 1], sems_1[c] + 2 + d, at_x(d))

    def plane_second(c):
        for d in range(1, 4):
            arrived(b.in_a1.at[c, d - 1], sems_1[c] + d - 1)
            arrived(b.in_b1.at[c, d - 1], sems_1[c] + 2 + d)
        sum_a = b.grads[c, :, tile16(y), LOW].astype(F32)
        sum_b = b.grads[c, :, tile16(x), HIGH].astype(F32)
        for d in range(3):
            sum_a += b.in_a1[c, d].astype(F32)
            sum_b += b.in_b1[c, d].astype(F32)
        b.sum_a1[c] = sum_a.astype(BF16)
        b.sum_b1[c] = sum_b.astype(BF16)
        for d in range(1, 4):
            to_y, to_x = lax.rem(y + d, 4), lax.rem(x + d, 4)
            push(b.sum_a1.at[c, :, :, tile128(to_x)], b.in_a2.at[c, d - 1], sems_2[c] + d - 1, at_x(d))
            push(b.sum_b1.at[c, :, :, tile128(to_y)], b.in_b2.at[c, d - 1], sems_2[c] + 2 + d, at_y(d))

    def plane_last(c):
        for d in range(1, 4):
            arrived(b.in_a2.at[c, d - 1], sems_2[c] + d - 1)
            arrived(b.in_b2.at[c, d - 1], sems_2[c] + 2 + d)
        sum_a = b.sum_a1[c, :, :, tile128(x)].astype(F32)
        sum_b = b.sum_b1[c, :, :, tile128(y)].astype(F32)
        for d in range(3):
            sum_a += b.in_a2[c, d].astype(F32)
            sum_b += b.in_b2[c, d].astype(F32)
        b.plane[:, c, 0] = sum_a.astype(BF16)
        b.plane[:, c, 1] = sum_b.astype(BF16)

    part_sem = take(3)

    def after_forward():
        for c in (3, 2):
            plane_first(c)
        for d in range(1, 4):
            push(b.part.at[lax.rem(r + d, 4)], b.part_in.at[d - 1], part_sem + d - 1, mate(d))

    attention(grp, b.normed, b.w, b.cot, b.grads, b.part, s, after_forward)
    for c in (0, 1):
        plane_first(c)
    for c in (3, 2, 0, 1):
        plane_second(c)
    for c in (3, 2, 0, 1):
        plane_last(c)

    column_sem = take(7)
    for d in range(1, 8):
        there = lax.div(lax.rem(g + 4 * d, 32), 16)
        push(b.plane.at[SHARD_AT[d], pl.ds(there * 2, 2)], b.in_z.at[d - 1], column_sem + d - 1, at_col(g + 4 * d))

    out = dot(b.nodes[r + 2], inputs.enc[...]) + b.part[r].astype(F32)
    for d in range(3):
        arrived(b.part_in.at[d], part_sem + d)
        out += b.part_in[d].astype(F32)
    layer_out[0] = out.astype(BF16)

    total = b.plane[0, pl.ds(hi * 2, 2)].astype(F32)
    for d in range(7):
        arrived(b.in_z.at[d], column_sem + d)
        total += b.in_z[d].astype(F32)
    b.total[pl.ds(hi * 2, 2)] = total.astype(BF16)
    far_sem = take()
    half = b.total.at[pl.ds(hi * 2, 2)]
    push(half, half, far_sem, at_col(g + 16))
    arrived(b.total.at[pl.ds(2 - hi * 2, 2)], far_sem)

    b.gathered[:, piece_a[0], piece_a[1]] = b.total[:, 0]
    b.gathered[:, piece_b[0], piece_b[1]] = b.total[:, 1]
    last_1, last_2 = take(6), take(6)
    for d in range(1, 4):
        part_a, part_b = b.gathered.at[(ALL,) + piece_a], b.gathered.at[(ALL,) + piece_b]
        push(part_a, part_a, last_1 + d - 1, at_x(d))
        push(part_b, part_b, last_1 + 2 + d, at_y(d))
    for d in range(1, 4):
        arrived(b.gathered.at[(ALL,) + piece_a], last_1 + d - 1)
        arrived(b.gathered.at[(ALL,) + piece_b], last_1 + 2 + d)
    for d in range(1, 4):
        part_a, part_b = b.gathered.at[(ALL,) + row_a], b.gathered.at[(ALL,) + row_b]
        push(part_a, part_a, last_2 + d - 1, at_y(d))
        push(part_b, part_b, last_2 + 2 + d, at_x(d))
    for d in range(1, 4):
        arrived(b.gathered.at[(ALL,) + row_a], last_2 + d - 1)
        arrived(b.gathered.at[(ALL,) + row_b], last_2 + 2 + d)
    grad_qkv[...] = b.gathered[0:3].astype(F32)
    grad_out[...] = b.gathered[3].astype(F32)
    for copy in started:
        copy.wait_send()
    assert used[0] <= SEMS and len(started) <= SEMS


def on_device(
    grid_fields, edge_grid, edge_count, edge_weight, enc_weight, qkv_weight, out_weight, cotangent
):
    vmem, anywhere = pl.BlockSpec(memory_space=pltpu.VMEM), pl.BlockSpec(memory_space=pl.ANY)
    return pl.pallas_call(
        step_kernel,
        out_shape=(
            jax.ShapeDtypeStruct((1, 128, 1024), BF16),
            jax.ShapeDtypeStruct((3, 64, 1024), F32),
            jax.ShapeDtypeStruct((64, 1024), F32),
        ),
        in_specs=[anywhere, vmem, vmem, vmem, vmem, anywhere, anywhere, anywhere],
        out_specs=(vmem, vmem, vmem),
        scratch_shapes=[
            *EXCHANGE.values(),
            *ATTENTION.values(),
            pltpu.SemaphoreType.DMA((SEMS,)),
            pltpu.SemaphoreType.DMA((SEMS,)),
            pltpu.SemaphoreType.DMA((4,)),
        ],
        compiler_params=pltpu.CompilerParams(
            collective_id=0, has_side_effects=True, vmem_limit_bytes=56 * 1024 * 1024
        ),
    )(
        grid_fields.reshape(GRID_DEV, 128),
        edge_grid,
        edge_count.reshape(1, 128),
        edge_weight,
        enc_weight,
        qkv_weight,
        out_weight,
        cotangent.reshape(128, 1024),
    )


def solution(mesh):
    placed = (
        P("member", "mp", None),
        P("mp", None),
        P("mp"),
        P("mp", None),
        P(),
        P(None, "mp", None),
        P("mp", None),
        P("member", "mp", None),
    )
    return jax.shard_map(
        on_device,
        mesh=mesh,
        in_specs=placed,
        out_specs=(P("member", "mp", None), P(None, "mp", None), P("mp", None)),
        check_vma=False,
    )
```

```python
import functools
import math

import jax
import jax.numpy as jnp
from jax import lax
from jax.experimental import pallas as pl
from jax.experimental.pallas import tpu as pltpu
from jax.sharding import PartitionSpec as P

MESH = pl.DeviceIdType.MESH
BF16, F32 = jnp.bfloat16, jnp.float32
LOG2E = math.log2(math.e)

GRID_DEV = 1728
EXT = 41 * 128
BAND = 17 * 128
KEYS = 768
NT = (((1,), (1,)), ((), ()))


def dot(a, b):
    return jnp.dot(a, b, preferred_element_type=F32)


def dot_nt(a, b):
    return lax.dot_general(a, b, NT, preferred_element_type=F32)


def attention_scratch():
    return dict(
        keys=pltpu.VMEM((1024, 256), BF16),
        keys_t=pltpu.VMEM((256, 1024), BF16),
        values=pltpu.VMEM((1024, 256), BF16),
        values_t=pltpu.VMEM((256, 1024), BF16),
        query=pltpu.VMEM((512, 256), BF16),
        query_tz=pltpu.VMEM((4, 128, 512), BF16),
        d_att_t=pltpu.VMEM((256, 512), BF16),
        bias=pltpu.VMEM((2, KEYS, 256), F32),
        weights=pltpu.VMEM((8, KEYS, 256), BF16),
        row_d=pltpu.VMEM((8, 1, 256), F32),
        d_att_z=pltpu.VMEM((8, 128, 256), BF16),
        att_t=pltpu.VMEM((256, 512), BF16),
        att=pltpu.VMEM((512, 256), BF16),
        d_query_t=pltpu.VMEM((256, 512), BF16),
        d_keys=pltpu.VMEM((1024, 256), F32),
        d_values=pltpu.VMEM((1024, 256), F32),
        left=pltpu.VMEM((256, 1024), BF16),
    )


def weight_grad(grads, c, left, right):
    def tile(t, carry):
        cols = pl.ds(pl.multiple_of(t * 256, 256), 256)
        product = dot(left(), right(cols)).astype(BF16)
        for j in range(4):
            grads[c, j, :, cols] = product[j * 64 : (j + 1) * 64]
        return carry

    lax.fori_loop(0, 4, tile, 0)


def attention(grp, normed, w, cot, grads, part, s, hooks):
    key_pos = lax.broadcasted_iota(jnp.int32, (KEYS, 256), 0)
    query_pos = lax.broadcasted_iota(jnp.int32, (KEYS, 256), 1)
    for qb in range(2):
        node = key_pos + (grp * 512 - 256 + qb * 256)
        inside = (key_pos >= query_pos) & (key_pos <= query_pos + 512) & (node >= 0) & (node < 2048)
        s.bias[qb] = jnp.where(inside, 0.0, -1e30)
    s.d_keys[...] = jnp.zeros_like(s.d_keys)
    s.d_values[...] = jnp.zeros_like(s.d_values)

    wq = w[:, 0].reshape(256, 1024)
    wk = w[:, 1].reshape(256, 1024)
    wv = w[:, 2].reshape(256, 1024)

    def project(t, carry):
        rows = pl.ds(pl.multiple_of(t * 256, 256), 256)
        block = normed[rows, :]
        s.keys[rows, :] = dot_nt(block, wk).astype(BF16)
        s.values[rows, :] = dot_nt(block, wv).astype(BF16)
        s.keys_t[:, rows] = dot_nt(wk, block).astype(BF16)
        s.values_t[:, rows] = dot_nt(wv, block).astype(BF16)
        return carry

    lax.fori_loop(0, 4, project, 0)

    def project_own(t, carry):
        rows = pl.ds(pl.multiple_of(t * 256, 256), 256)
        block = normed[pl.ds(pl.multiple_of(t * 256 + 256, 256), 256), :]
        s.query[rows, :] = (dot_nt(block, wq) * (LOG2E / 8)).astype(BF16)
        query_t = dot_nt(wq, block) * (LOG2E / 8)
        upper = lax.broadcasted_iota(jnp.int32, (128, 256), 0) < 64
        for h in range(4):
            pair = query_t[h // 2 * 128 : h // 2 * 128 + 128]
            keep = upper if h % 2 == 0 else ~upper
            s.query_tz[h, :, rows] = jnp.where(keep, pair, 0.0).astype(BF16)
        return carry

    lax.fori_loop(0, 2, project_own, 0)
    hooks.before_out()
    wo = w[:, 3].reshape(256, 1024)

    def project_cot(t, carry):
        rows = pl.ds(pl.multiple_of(t * 256, 256), 256)
        cot_rows = cot[pl.ds(t * 2, 2)].reshape(256, 1024)
        s.d_att_t[:, rows] = dot_nt(wo, cot_rows).astype(BF16)
        return carry

    lax.fori_loop(0, 2, project_cot, 0)

    def place(i):
        pair, qb = lax.div(i, 2), lax.rem(i, 2)
        key_rows = pl.ds(pl.multiple_of(qb * 256, 256), KEYS)
        lanes = pl.ds(pl.multiple_of(pair * 128, 128), 128)
        cols = pl.ds(pl.multiple_of(qb * 256, 256), 256)
        return pair, qb, key_rows, lanes, cols

    def head_rows(pair, hh):
        return pl.ds(pl.multiple_of(pair * 128 + hh * 64, 64), 64)

    def forward(i, carry):
        pair, qb, key_rows, lanes, cols = place(i)
        key_block = s.keys[key_rows, lanes]
        all_weights, scaled, outs = [], [], []
        for hh in range(2):
            scores = dot(key_block, s.query_tz[pair * 2 + hh, :, cols]) + s.bias[qb]
            weight = jnp.exp2(scores - jnp.max(scores, axis=0, keepdims=True))
            inverse = 1.0 / jnp.sum(weight, axis=0, keepdims=True)
            weight = weight.astype(BF16)
            s.weights[i * 2 + hh] = weight
            all_weights.append(weight)
            rows = head_rows(pair, hh)
            out = dot(s.values_t[rows, key_rows], weight) * inverse
            d_out = s.d_att_t[rows, cols].astype(F32)
            s.row_d[i * 2 + hh] = jnp.sum(d_out * out, axis=0, keepdims=True) * inverse
            s.att_t[rows, cols] = out.astype(BF16)
            outs.append(out)
            scaled.append(d_out * inverse)
        s.att[cols, lanes] = jnp.concatenate(outs, axis=0).T.astype(BF16)
        both = jnp.concatenate(scaled, axis=0)
        upper = lax.broadcasted_iota(jnp.int32, (128, 256), 0) < 64
        s.d_att_z[i * 2] = jnp.where(upper, both, 0.0).astype(BF16)
        s.d_att_z[i * 2 + 1] = jnp.where(upper, 0.0, both).astype(BF16)
        rows_form = both.T
        low = lax.broadcasted_iota(jnp.int32, (256, 128), 1) < 64
        s.d_values[key_rows, lanes] += dot(
            all_weights[0], jnp.where(low, rows_form, 0.0).astype(BF16)
        ) + dot(all_weights[1], jnp.where(low, 0.0, rows_form).astype(BF16))
        return carry

    lax.fori_loop(0, 4, forward, 0)

    def project_out(t, carry):
        cols = pl.ds(pl.multiple_of(t * 256, 256), 256)
        product = dot(s.att[...], w[:, 3, :, cols].reshape(256, 256)).astype(BF16)
        for k in range(4):
            part[k, :, cols] = product[k * 128 : (k + 1) * 128]
        return carry

    lax.fori_loop(0, 4, project_out, 0)
    hooks.have_part()
    weight_grad(grads, 3, lambda: s.att_t[...], lambda cols: cot[:, :, cols].reshape(512, 256))
    hooks.have_grad(3)
    s.left[...] = s.d_values[...].T.astype(BF16)
    weight_grad(grads, 2, lambda: s.left[...], lambda cols: normed[:, cols])
    hooks.have_grad(2)

    def backward(i, carry):
        pair, qb, key_rows, lanes, cols = place(i)
        value_block = s.values[key_rows, lanes]
        low = lax.broadcasted_iota(jnp.int32, (256, 128), 1) < 64
        query = s.query[cols, lanes]
        d_keys = jnp.zeros((KEYS, 128), F32)
        for hh in range(2):
            d_weight = dot(value_block, s.d_att_z[i * 2 + hh])
            d_scores = (s.weights[i * 2 + hh].astype(F32) * (d_weight - s.row_d[i * 2 + hh])).astype(BF16)
            rows = head_rows(pair, hh)
            s.d_query_t[rows, cols] = (dot(s.keys_t[rows, key_rows], d_scores) * 0.125).astype(BF16)
            d_keys += dot(d_scores, jnp.where(low if hh == 0 else ~low, query, jnp.zeros_like(query)))
        s.d_keys[key_rows, lanes] += d_keys * (1.0 / LOG2E)
        return carry

    lax.fori_loop(0, 4, backward, 0)
    hooks.after_backward()
    weight_grad(grads, 0, lambda: s.d_query_t[...], lambda cols: normed[256:768, cols])
    hooks.have_grad(0)
    s.left[...] = s.d_keys[...].T.astype(BF16)
    weight_grad(grads, 1, lambda: s.left[...], lambda cols: normed[:, cols])
    hooks.have_grad(1)


class Names:
    def __init__(self, names, refs):
        self.__dict__.update(zip(names, refs, strict=True))


def exchange_scratch():
    return dict(
        ext=pltpu.VMEM((EXT, 128), BF16),
        place=pltpu.VMEM((128, EXT), BF16),
        coef=pltpu.VMEM((128, 32), F32),
        nodes=pltpu.VMEM((8, 128, 128), BF16),
        normed=pltpu.VMEM((1024, 1024), BF16),
        w=pltpu.VMEM((4, 4, 64, 1024), BF16),
        cot=pltpu.VMEM((4, 128, 1024), BF16),
        grads=pltpu.VMEM((4, 4, 64, 1024), BF16),
        part=pltpu.VMEM((4, 128, 1024), BF16),
        part_in=pltpu.VMEM((3, 128, 1024), BF16),
        in_a1=pltpu.VMEM((4, 3, 4, 16, 512), BF16),
        in_b1=pltpu.VMEM((4, 3, 4, 16, 512), BF16),
        sum_a1=pltpu.VMEM((4, 4, 16, 512), BF16),
        sum_b1=pltpu.VMEM((4, 4, 16, 512), BF16),
        in_a2=pltpu.VMEM((4, 3, 4, 16, 128), BF16),
        in_b2=pltpu.VMEM((4, 3, 4, 16, 128), BF16),
        plane=pltpu.VMEM((4, 4, 2, 16, 128), BF16),
        in_z=pltpu.VMEM((2, 4, 2, 16, 128), BF16),
        in_z4=pltpu.VMEM((2, 4, 16, 128), BF16),
        half_sum=pltpu.VMEM((4, 2, 16, 128), BF16),
        far=pltpu.VMEM((4, 2, 16, 128), BF16),
        gathered=pltpu.VMEM((4, 64, 1024), BF16),
        out=pltpu.VMEM((128, 1024), BF16),
        edge=pltpu.VMEM((32, 128), jnp.int32),
        count=pltpu.VMEM((1, 128), jnp.int32),
        edge_w=pltpu.VMEM((32, 128), F32),
        enc=pltpu.VMEM((128, 1024), BF16),
        index=pltpu.VMEM((128, 32), jnp.int32),
    )


EXCHANGE = exchange_scratch()
ATTENTION = attention_scratch()
SEMS = 128
ALL = slice(None)
LOW, HIGH = pl.ds(0, 512), pl.ds(512, 512)


def tile16(k):
    return pl.ds(pl.multiple_of(k * 16, 16), 16)


def tile128(k):
    return pl.ds(pl.multiple_of(k * 128, 128), 128)


def step_kernel(*refs):
    inputs = Names(("grid", "edge", "count", "edge_w", "enc", "wqkv", "wo", "cot"), refs[:8])
    layer_out, weight_grads = refs[8:10]
    b = Names(tuple(EXCHANGE), refs[10 : 10 + len(EXCHANGE)])
    s = Names(tuple(ATTENTION), refs[10 + len(EXCHANGE) : 10 + len(EXCHANGE) + len(ATTENTION)])
    send_sem, recv_sem, local_sem = refs[10 + len(EXCHANGE) + len(ATTENTION) :]

    member, mp = lax.axis_index("member"), lax.axis_index("mp")
    x, hi, y = lax.div(member, 8), lax.rem(lax.div(member, 4), 2), lax.rem(member, 4)
    g = hi * 16 + mp
    r, grp = lax.rem(mp, 4), lax.div(mp, 4)

    def at_col(place):
        there = lax.rem(place + 32, 32)
        return (x * 8 + lax.div(there, 16) * 4 + y, lax.rem(there, 16))

    def at_x(d):
        return (lax.rem(x + d, 4) * 8 + hi * 4 + y, mp)

    def at_y(d):
        return (x * 8 + hi * 4 + lax.rem(y + d, 4), mp)

    def mate(d):
        return at_col(g - r + lax.rem(r + d, 4))

    started, used, local = [], [0], [0]

    def take(n=1):
        used[0] += n
        return used[0] - n

    def push(src, dst, recv, device):
        copy = pltpu.make_async_remote_copy(
            src_ref=src,
            dst_ref=dst,
            send_sem=send_sem.at[len(started)],
            recv_sem=recv_sem.at[recv],
            device_id=device,
            device_id_type=MESH,
        )
        copy.start()
        started.append(copy)

    def arrived(dst, recv):
        pltpu.make_async_copy(dst, dst, recv_sem.at[recv]).wait()

    def here(src, dst):
        copy = pltpu.make_async_copy(src, dst, local_sem.at[local[0]])
        local[0] += 1
        copy.start()
        return copy

    barrier = pltpu.get_barrier_semaphore()
    sources = [at_col(g + 4 * d) for d in (1, -1, 2, -2)]
    sources += [at_x(d) for d in range(1, 4)] + [at_y(d) for d in range(1, 4)]
    sources += [mate(d) for d in range(1, 4)]
    sources += [at_col(g - r + d) for d in (-2, -1, 4, 5)]
    for device in sources:
        pl.semaphore_signal(barrier, inc=1, device_id=device, device_id_type=MESH)
    own_w = here(inputs.wqkv, b.w.at[0, pl.ds(0, 3)])
    own_wo = here(inputs.wo, b.w.at[0, 3])
    edges = [here(getattr(inputs, n), getattr(b, n)) for n in ("edge", "count", "edge_w")]
    own_enc = here(inputs.enc, b.enc)
    own_grid = here(inputs.grid, b.ext.at[pl.ds(GRID_DEV, GRID_DEV)])
    own_cot = here(inputs.cot, b.cot.at[r])
    pl.semaphore_wait(barrier, len(sources))

    own_w.wait()
    own_wo.wait()
    piece_a = (tile16(y), tile128(x))
    piece_b = (tile16(x), tile128(y + 4))
    z_sem = take(6)
    for n, (j, off_a, off_b) in enumerate(((1, 4, 4), (2, -4, -4), (3, 8, -8))):
        push(b.w.at[(0, ALL) + piece_a], b.w.at[(j, ALL) + piece_a], z_sem + n, at_col(g + off_a))
        push(b.w.at[(0, ALL) + piece_b], b.w.at[(j, ALL) + piece_b], z_sem + 3 + n, at_col(g + off_b))

    left_rows, right_rows = pl.ds(0, GRID_DEV), pl.ds(2 * GRID_DEV, GRID_DEV)
    grid_sem = take(2)
    push(inputs.grid, b.ext.at[left_rows], grid_sem, at_col(g + 1))
    push(inputs.grid, b.ext.at[right_rows], grid_sem + 1, at_col(g - 1))

    b.place[...] = jnp.zeros_like(b.place)
    b.ext[pl.ds(3 * GRID_DEV, EXT - 3 * GRID_DEV), :] = jnp.zeros((EXT - 3 * GRID_DEV, 128), BF16)
    for copy in edges:
        copy.wait()
    slot = lax.broadcasted_iota(jnp.int32, (32, 128), 0)
    coef = jnp.where(slot < b.count[...], b.edge_w[...], 0.0)
    index = (b.edge[...] - (mp - 1) * GRID_DEV).astype(F32)
    both = jnp.concatenate([coef, index, jnp.zeros((64, 128), F32)], axis=0).T
    b.coef[...] = both[:, 0:32]
    b.index[...] = both[:, 32:64].astype(jnp.int32)

    def build(k, carry):
        rows = tile16(k)
        start = pl.multiple_of(lax.div(862 + 216 * k, 128) * 128, 128)
        index = b.index[rows, :] - start
        coef = b.coef[rows, :]
        lane = lax.broadcasted_iota(jnp.int32, (16, BAND), 1)
        total = jnp.zeros((16, BAND), F32)
        for e in range(32):
            total += jnp.where(lane == index[:, e : e + 1], coef[:, e : e + 1], 0.0)
        b.place[rows, pl.ds(start, BAND)] = total.astype(BF16)
        return carry

    lax.fori_loop(0, 8, build, 0)

    others = pl.ds(1, 3)
    for n in range(3):
        arrived(b.w.at[(n + 1, ALL) + piece_a], z_sem + n)
        arrived(b.w.at[(n + 1, ALL) + piece_b], z_sem + 3 + n)
    first_a, first_b = take(3), take(3)
    for d in range(1, 4):
        part_a = b.w.at[(others, ALL) + piece_a]
        part_b = b.w.at[(others, ALL) + piece_b]
        push(part_a, part_a, first_a + d - 1, at_x(d))
        push(part_b, part_b, first_b + d - 1, at_y(d))

    own_grid.wait()
    arrived(b.ext.at[left_rows], grid_sem)
    arrived(b.ext.at[right_rows], grid_sem + 1)
    node_in = dot(b.place[...], b.ext[...]).astype(BF16)
    b.nodes[pl.ds(r + 2, 1)] = node_in[None]
    mine = b.nodes.at[r + 2]
    mate_sem, next_sem = take(3), take(4)
    near = jnp.where(r < 2, g - r - 4, g - r + 4)
    for d in range(1, 4):
        push(mine, mine, mate_sem + d - 1, mate(d))
    for t in range(4):
        push(mine, b.nodes.at[lax.rem(r + 6, 8)], next_sem + r, at_col(near + t))

    for d in range(1, 4):
        arrived(b.w.at[(others, ALL) + piece_a], first_a + d - 1)
        arrived(b.w.at[(others, ALL) + piece_b], first_b + d - 1)
    row_a = (tile16(y), LOW)
    row_b = (tile16(x), HIGH)
    QKV, OUT = pl.ds(0, 3), pl.ds(3, 1)
    second = {}
    for kinds, name in ((QKV, "qkv"), (OUT, "out")):
        second[name] = take(6)
        for d in range(1, 4):
            part_a = b.w.at[(others, kinds) + row_a]
            part_b = b.w.at[(others, kinds) + row_b]
            push(part_a, part_a, second[name] + d - 1, at_y(d))
            push(part_b, part_b, second[name] + 2 + d, at_x(d))

    def wait_second(kinds, name):
        for d in range(1, 4):
            arrived(b.w.at[(others, kinds) + row_a], second[name] + d - 1)
            arrived(b.w.at[(others, kinds) + row_b], second[name] + 2 + d)

    own_cot.wait()
    cot_sem = take(3)
    sibling = r + 1 - 2 * lax.rem(r, 2)
    across = lax.rem(r + 2, 4)
    push(b.cot.at[r], b.cot.at[r], cot_sem, at_col(g - r + across))
    push(b.cot.at[r], b.cot.at[r], cot_sem + 1, at_col(g - r + sibling))

    for d in range(1, 4):
        arrived(mine, mate_sem + d - 1)
    for t, place in enumerate((6, 7, 0, 1)):
        arrived(b.nodes.at[place], next_sem + t)
    own_enc.wait()

    def normalise(k, carry):
        hidden = dot(b.nodes[k], b.enc[...])
        centred = hidden - jnp.mean(hidden, axis=1, keepdims=True)
        spread = jnp.mean(centred * centred, axis=1, keepdims=True)
        b.normed[tile128(k), :] = (centred * lax.rsqrt(spread + 1e-05)).astype(BF16)
        return carry

    lax.fori_loop(0, 8, normalise, 0)

    arrived(b.cot.at[across], cot_sem)
    push(b.cot.at[across], b.cot.at[across], cot_sem + 2, at_col(g - r + sibling))
    wait_second(QKV, "qkv")

    sems_1 = [take(6) for _ in range(4)]
    sems_2 = [take(6) for _ in range(4)]
    part_sem = take(3)

    def plane_first(c):
        for d in range(1, 4):
            to_y, to_x = lax.rem(y + d, 4), lax.rem(x + d, 4)
            push(b.grads.at[c, :, tile16(to_y), LOW], b.in_a1.at[c, d - 1], sems_1[c] + d - 1, at_y(d))
            push(b.grads.at[c, :, tile16(to_x), HIGH], b.in_b1.at[c, d - 1], sems_1[c] + 2 + d, at_x(d))

    def plane_second(c):
        for d in range(1, 4):
            arrived(b.in_a1.at[c, d - 1], sems_1[c] + d - 1)
            arrived(b.in_b1.at[c, d - 1], sems_1[c] + 2 + d)
        sum_a = b.grads[c, :, tile16(y), LOW].astype(F32)
        sum_b = b.grads[c, :, tile16(x), HIGH].astype(F32)
        for d in range(3):
            sum_a += b.in_a1[c, d].astype(F32)
            sum_b += b.in_b1[c, d].astype(F32)
        b.sum_a1[c] = sum_a.astype(BF16)
        b.sum_b1[c] = sum_b.astype(BF16)
        for d in range(1, 4):
            to_y, to_x = lax.rem(y + d, 4), lax.rem(x + d, 4)
            push(b.sum_a1.at[c, :, :, tile128(to_x)], b.in_a2.at[c, d - 1], sems_2[c] + d - 1, at_x(d))
            push(b.sum_b1.at[c, :, :, tile128(to_y)], b.in_b2.at[c, d - 1], sems_2[c] + 2 + d, at_y(d))

    def plane_last(c):
        for d in range(1, 4):
            arrived(b.in_a2.at[c, d - 1], sems_2[c] + d - 1)
            arrived(b.in_b2.at[c, d - 1], sems_2[c] + 2 + d)
        sum_a = b.sum_a1[c, :, :, tile128(x)].astype(F32)
        sum_b = b.sum_b1[c, :, :, tile128(y)].astype(F32)
        for d in range(3):
            sum_a += b.in_a2[c, d].astype(F32)
            sum_b += b.in_b2[c, d].astype(F32)
        b.plane[:, c, 0] = sum_a.astype(BF16)
        b.plane[:, c, 1] = sum_b.astype(BF16)

    class Column:
        def __init__(self, first):
            self.c = pl.ds(first, 2)
            self.near, self.far, self.one, self.two = take(4), take(), take(6), take(6)

        def to_owners(self):
            c = self.c
            push(b.plane.at[1, c], b.in_z.at[0, c], self.near, at_col(g - 4))
            push(b.plane.at[2, c], b.in_z.at[1, c], self.near + 1, at_col(g + 4))
            push(b.plane.at[3, c, 0], b.in_z4.at[0, c], self.near + 2, at_col(g + 8))
            push(b.plane.at[3, c, 1], b.in_z4.at[1, c], self.near + 3, at_col(g - 8))

        def to_far(self):
            c = self.c
            for n in range(2):
                arrived(b.in_z.at[n, c], self.near + n)
                arrived(b.in_z4.at[n, c], self.near + 2 + n)
            for n in range(2):
                total = b.plane[0, c, n].astype(F32) + b.in_z4[n, c].astype(F32)
                total += b.in_z[0, c, n].astype(F32) + b.in_z[1, c, n].astype(F32)
                b.half_sum[c, n] = total.astype(BF16)
            push(b.half_sum.at[c], b.far.at[c], self.far, at_col(g + 16))

        def to_plane(self):
            c = self.c
            arrived(b.far.at[c], self.far)
            total = (b.half_sum[c].astype(F32) + b.far[c].astype(F32)).astype(BF16)
            b.gathered[c, piece_a[0], piece_a[1]] = total[:, 0]
            b.gathered[c, piece_b[0], piece_b[1]] = total[:, 1]
            for d in range(1, 4):
                part_a, part_b = b.gathered.at[(c,) + piece_a], b.gathered.at[(c,) + piece_b]
                push(part_a, part_a, self.one + d - 1, at_x(d))
                push(part_b, part_b, self.one + 2 + d, at_y(d))

        def to_rest(self):
            c = self.c
            for d in range(1, 4):
                arrived(b.gathered.at[(c,) + piece_a], self.one + d - 1)
                arrived(b.gathered.at[(c,) + piece_b], self.one + 2 + d)
            for d in range(1, 4):
                part_a, part_b = b.gathered.at[(c,) + row_a], b.gathered.at[(c,) + row_b]
                push(part_a, part_a, self.two + d - 1, at_y(d))
                push(part_b, part_b, self.two + 2 + d, at_x(d))

        def finish(self):
            c = self.c
            for d in range(1, 4):
                arrived(b.gathered.at[(c,) + row_a], self.two + d - 1)
                arrived(b.gathered.at[(c,) + row_b], self.two + 2 + d)
            return here(b.gathered.at[c], weight_grads.at[c])

    early, late = Column(2), Column(0)

    class Hooks:
        def before_out(self):
            wait_second(OUT, "out")
            arrived(b.cot.at[sibling], cot_sem + 1)
            arrived(b.cot.at[lax.rem(sibling + 2, 4)], cot_sem + 2)

        def have_part(self):
            for d in range(1, 4):
                push(b.part.at[lax.rem(r + d, 4)], b.part_in.at[d - 1], part_sem + d - 1, mate(d))

        def have_grad(self, c):
            plane_first(c)

        def after_backward(self):
            plane_second(3)
            plane_second(2)

    attention(grp, b.normed, b.w, b.cot, b.grads, b.part, s, Hooks())

    plane_last(3)
    plane_last(2)
    early.to_owners()
    out = dot(b.nodes[r + 2], b.enc[...]) + b.part[r].astype(F32)
    for d in range(3):
        arrived(b.part_in.at[d], part_sem + d)
        out += b.part_in[d].astype(F32)
    b.out[...] = out.astype(BF16)
    results = [here(b.out, layer_out)]
    plane_second(0)
    plane_second(1)
    early.to_far()
    plane_last(0)
    plane_last(1)
    late.to_owners()
    early.to_plane()
    late.to_far()
    early.to_rest()
    late.to_plane()
    results.append(early.finish())
    late.to_rest()
    results.append(late.finish())
    for copy in results:
        copy.wait()
    for copy in started:
        copy.wait_send()
    assert used[0] <= SEMS and len(started) <= SEMS and local[0] <= 16


def finish_kernel(layer_in, grads, layer_out, grad_qkv, grad_out):
    layer_out[...] = layer_in[...]
    grad_qkv[...] = grads[0:3].astype(F32)
    grad_out[...] = grads[3].astype(F32)


def on_device(
    grid_fields, edge_grid, edge_count, edge_weight, enc_weight, qkv_weight, out_weight, cotangent
):
    vmem, anywhere = pl.BlockSpec(memory_space=pltpu.VMEM), pl.BlockSpec(memory_space=pl.ANY)
    layer_out, grads = pl.pallas_call(
        step_kernel,
        out_shape=(
            jax.ShapeDtypeStruct((128, 1024), BF16),
            jax.ShapeDtypeStruct((4, 64, 1024), BF16),
        ),
        in_specs=[anywhere] * 8,
        out_specs=(anywhere, anywhere),
        scratch_shapes=[
            *EXCHANGE.values(),
            *ATTENTION.values(),
            pltpu.SemaphoreType.DMA((SEMS,)),
            pltpu.SemaphoreType.DMA((SEMS,)),
            pltpu.SemaphoreType.DMA((16,)),
        ],
        compiler_params=pltpu.CompilerParams(
            collective_id=0, has_side_effects=True, vmem_limit_bytes=56 * 1024 * 1024
        ),
    )(
        grid_fields.reshape(GRID_DEV, 128),
        edge_grid.T,
        edge_count.reshape(1, 128),
        edge_weight.T,
        enc_weight,
        qkv_weight,
        out_weight,
        cotangent.reshape(128, 1024),
    )
    layer_out, grad_qkv, grad_out = pl.pallas_call(
        finish_kernel,
        out_shape=(
            jax.ShapeDtypeStruct((128, 1024), BF16),
            jax.ShapeDtypeStruct((3, 64, 1024), F32),
            jax.ShapeDtypeStruct((64, 1024), F32),
        ),
        in_specs=[vmem, vmem],
        out_specs=(vmem, vmem, vmem),
    )(layer_out, grads)
    return layer_out[None], grad_qkv, grad_out


def solution(mesh):
    placed = (
        P("member", "mp", None),
        P("mp", None),
        P("mp"),
        P("mp", None),
        P(),
        P(None, "mp", None),
        P("mp", None),
        P("member", "mp", None),
    )
    return jax.shard_map(
        on_device,
        mesh=mesh,
        in_specs=placed,
        out_specs=(P("member", "mp", None), P(None, "mp", None), P("mp", None)),
        check_vma=False,
    )
```

```python
import functools
import math

import jax
import jax.numpy as jnp
from jax import lax
from jax.experimental import pallas as pl
from jax.experimental.pallas import tpu as pltpu
from jax.sharding import PartitionSpec as P

MESH = pl.DeviceIdType.MESH
BF16, F32 = jnp.bfloat16, jnp.float32
LOG2E = math.log2(math.e)

GRID_DEV = 1728
EXT = 41 * 128
BAND = 17 * 128
KEYS = 768
NT = (((1,), (1,)), ((), ()))
SHARD_AT = {1: 2, 2: 3, 3: 1, 4: 0, 5: 2, 6: 3, 7: 1}


def dot(a, b):
    return jnp.dot(a, b, preferred_element_type=F32)


def dot_nt(a, b):
    return lax.dot_general(a, b, NT, preferred_element_type=F32)


def attention_scratch():
    return dict(
        keys=pltpu.VMEM((1024, 256), BF16),
        keys_t=pltpu.VMEM((256, 1024), BF16),
        values=pltpu.VMEM((1024, 256), BF16),
        values_t=pltpu.VMEM((256, 1024), BF16),
        query=pltpu.VMEM((512, 256), BF16),
        query_tz=pltpu.VMEM((4, 128, 512), BF16),
        d_att_t=pltpu.VMEM((256, 512), BF16),
        bias=pltpu.VMEM((2, KEYS, 256), F32),
        weights=pltpu.VMEM((8, KEYS, 256), BF16),
        row_d=pltpu.VMEM((8, 1, 256), F32),
        d_att_z=pltpu.VMEM((8, 128, 256), BF16),
        att_t=pltpu.VMEM((256, 512), BF16),
        att=pltpu.VMEM((512, 256), BF16),
        d_query_t=pltpu.VMEM((256, 512), BF16),
        d_keys=pltpu.VMEM((1024, 256), F32),
        d_values=pltpu.VMEM((1024, 256), F32),
        left=pltpu.VMEM((256, 1024), BF16),
    )


def weight_grad(grads, c, left, right):
    def tile(t, carry):
        cols = pl.ds(pl.multiple_of(t * 256, 256), 256)
        product = dot(left(), right(cols)).astype(BF16)
        for j in range(4):
            grads[c, j, :, cols] = product[j * 64 : (j + 1) * 64]
        return carry

    lax.fori_loop(0, 4, tile, 0, unroll=True)


def project_attended(w, s, part):
    def project_out(t, carry):
        cols = pl.ds(pl.multiple_of(t * 256, 256), 256)
        product = dot(s.att[...], w[:, 3, :, cols].reshape(256, 256)).astype(BF16)
        for k in range(4):
            part[k, :, cols] = product[k * 128 : (k + 1) * 128]
        return carry

    lax.fori_loop(0, 4, project_out, 0, unroll=True)


def attention(grp, normed, w, cot, grads, part, s, hooks):
    key_pos = lax.broadcasted_iota(jnp.int32, (KEYS, 256), 0)
    query_pos = lax.broadcasted_iota(jnp.int32, (KEYS, 256), 1)
    for qb in range(2):
        node = key_pos + (grp * 512 - 256 + qb * 256)
        inside = (key_pos >= query_pos) & (key_pos <= query_pos + 512) & (node >= 0) & (node < 2048)
        s.bias[qb] = jnp.where(inside, 0.0, -1e30)
    s.d_keys[...] = jnp.zeros_like(s.d_keys)
    s.d_values[...] = jnp.zeros_like(s.d_values)

    wk = w[:, 1].reshape(256, 1024)
    wv = w[:, 2].reshape(256, 1024)

    def project(t, carry):
        rows = pl.ds(pl.multiple_of(t * 256, 256), 256)
        block = normed[rows, :]
        s.keys[rows, :] = dot_nt(block, wk).astype(BF16)
        s.values[rows, :] = dot_nt(block, wv).astype(BF16)
        s.keys_t[:, rows] = dot_nt(wk, block).astype(BF16)
        s.values_t[:, rows] = dot_nt(wv, block).astype(BF16)
        return carry

    lax.fori_loop(0, 4, project, 0, unroll=True)
    hooks.before_query()
    wq = w[:, 0].reshape(256, 1024)

    def project_own(t, carry):
        rows = pl.ds(pl.multiple_of(t * 256, 256), 256)
        block = normed[pl.ds(pl.multiple_of(t * 256 + 256, 256), 256), :]
        s.query[rows, :] = (dot_nt(block, wq) * (LOG2E / 8)).astype(BF16)
        query_t = dot_nt(wq, block) * (LOG2E / 8)
        upper = lax.broadcasted_iota(jnp.int32, (128, 256), 0) < 64
        for h in range(4):
            pair = query_t[h // 2 * 128 : h // 2 * 128 + 128]
            keep = upper if h % 2 == 0 else ~upper
            s.query_tz[h, :, rows] = jnp.where(keep, pair, 0.0).astype(BF16)
        return carry

    lax.fori_loop(0, 2, project_own, 0, unroll=True)
    hooks.before_out()
    wo = w[:, 3].reshape(256, 1024)

    def project_cot(t, carry):
        rows = pl.ds(pl.multiple_of(t * 256, 256), 256)
        cot_rows = cot[pl.ds(t * 2, 2)].reshape(256, 1024)
        s.d_att_t[:, rows] = dot_nt(wo, cot_rows).astype(BF16)
        return carry

    lax.fori_loop(0, 2, project_cot, 0, unroll=True)

    def place(i):
        pair, qb = lax.div(i, 2), lax.rem(i, 2)
        key_rows = pl.ds(pl.multiple_of(qb * 256, 256), KEYS)
        lanes = pl.ds(pl.multiple_of(pair * 128, 128), 128)
        cols = pl.ds(pl.multiple_of(qb * 256, 256), 256)
        return pair, qb, key_rows, lanes, cols

    def head_rows(pair, hh):
        return pl.ds(pl.multiple_of(pair * 128 + hh * 64, 64), 64)

    def forward(i, carry):
        pair, qb, key_rows, lanes, cols = place(i)
        key_block = s.keys[key_rows, lanes]
        scaled, outs = [], []
        scores = [dot(key_block, s.query_tz[pair * 2 + hh, :, cols]) + s.bias[qb] for hh in range(2)]
        tops = [jnp.max(v, axis=0, keepdims=True) for v in scores]
        all_weights, inverses = [], []
        for hh in range(2):
            weight = jnp.exp2(scores[hh] - tops[hh])
            inverses.append(1.0 / jnp.sum(weight, axis=0, keepdims=True))
            all_weights.append(weight.astype(BF16))
            s.weights[i * 2 + hh] = all_weights[hh]
        for hh in range(2):
            rows = head_rows(pair, hh)
            inverse = inverses[hh]
            out = dot(s.values_t[rows, key_rows], all_weights[hh]) * inverse
            d_out = s.d_att_t[rows, cols].astype(F32)
            s.row_d[i * 2 + hh] = jnp.sum(d_out * out, axis=0, keepdims=True) * inverse
            s.att_t[rows, cols] = out.astype(BF16)
            outs.append(out)
            scaled.append(d_out * inverse)
        s.att[cols, lanes] = jnp.concatenate(outs, axis=0).T.astype(BF16)
        both = jnp.concatenate(scaled, axis=0)
        upper = lax.broadcasted_iota(jnp.int32, (128, 256), 0) < 64
        s.d_att_z[i * 2] = jnp.where(upper, both, 0.0).astype(BF16)
        s.d_att_z[i * 2 + 1] = jnp.where(upper, 0.0, both).astype(BF16)
        rows_form = both.T
        low = lax.broadcasted_iota(jnp.int32, (256, 128), 1) < 64
        s.d_values[key_rows, lanes] += dot(
            all_weights[0], jnp.where(low, rows_form, 0.0).astype(BF16)
        ) + dot(all_weights[1], jnp.where(low, 0.0, rows_form).astype(BF16))
        return carry

    lax.fori_loop(0, 4, forward, 0, unroll=True)

    weight_grad(grads, 3, lambda: s.att_t[...], lambda cols: cot[:, :, cols].reshape(512, 256))
    hooks.have_grad(3)
    s.left[...] = s.d_values[...].T.astype(BF16)
    weight_grad(grads, 2, lambda: s.left[...], lambda cols: normed[:, cols])
    hooks.have_grad(2)
    project_attended(w, s, part)
    hooks.have_part()

    def backward(i, carry):
        pair, qb, key_rows, lanes, cols = place(i)
        value_block = s.values[key_rows, lanes]
        low = lax.broadcasted_iota(jnp.int32, (256, 128), 1) < 64
        query = s.query[cols, lanes]
        d_keys = jnp.zeros((KEYS, 128), F32)
        for hh in range(2):
            d_weight = dot(value_block, s.d_att_z[i * 2 + hh])
            d_scores = (s.weights[i * 2 + hh].astype(F32) * (d_weight - s.row_d[i * 2 + hh])).astype(BF16)
            rows = head_rows(pair, hh)
            s.d_query_t[rows, cols] = (dot(s.keys_t[rows, key_rows], d_scores) * 0.125).astype(BF16)
            d_keys += dot(d_scores, jnp.where(low if hh == 0 else ~low, query, jnp.zeros_like(query)))
        s.d_keys[key_rows, lanes] += d_keys * (1.0 / LOG2E)
        return carry

    lax.fori_loop(0, 4, backward, 0, unroll=True)
    weight_grad(grads, 0, lambda: s.d_query_t[...], lambda cols: normed[256:768, cols])
    hooks.have_grad(0)
    s.left[...] = s.d_keys[...].T.astype(BF16)
    weight_grad(grads, 1, lambda: s.left[...], lambda cols: normed[:, cols])
    hooks.have_grad(1)


class Names:
    def __init__(self, names, refs):
        self.__dict__.update(zip(names, refs, strict=True))


def exchange_scratch():
    return dict(
        ext=pltpu.VMEM((EXT, 128), BF16),
        place=pltpu.VMEM((128, EXT), BF16),
        coef=pltpu.VMEM((128, 32), F32),
        nodes=pltpu.VMEM((8, 128, 128), BF16),
        normed=pltpu.VMEM((1024, 1024), BF16),
        w=pltpu.VMEM((4, 4, 64, 1024), BF16),
        cot=pltpu.VMEM((4, 128, 1024), BF16),
        grads=pltpu.VMEM((4, 4, 64, 1024), BF16),
        part=pltpu.VMEM((4, 128, 1024), BF16),
        part_in=pltpu.VMEM((3, 128, 1024), BF16),
        in_a1=pltpu.VMEM((4, 3, 4, 16, 512), BF16),
        in_b1=pltpu.VMEM((4, 3, 4, 16, 512), BF16),
        sum_a1=pltpu.VMEM((4, 4, 16, 512), BF16),
        sum_b1=pltpu.VMEM((4, 4, 16, 512), BF16),
        in_a2=pltpu.VMEM((3, 4, 4, 16, 128), BF16),
        in_b2=pltpu.VMEM((3, 4, 4, 16, 128), BF16),
        plane=pltpu.VMEM((4, 4, 2, 16, 128), BF16),
        in_z=pltpu.VMEM((8, 4, 2, 16, 128), BF16),
        gathered=pltpu.VMEM((4, 64, 1024), BF16),
        out=pltpu.VMEM((128, 1024), BF16),
        edge=pltpu.VMEM((32, 128), jnp.int32),
        count=pltpu.VMEM((1, 128), jnp.int32),
        edge_w=pltpu.VMEM((32, 128), F32),
        enc=pltpu.VMEM((128, 1024), BF16),
        index=pltpu.VMEM((128, 32), jnp.int32),
    )


EXCHANGE = exchange_scratch()
ATTENTION = attention_scratch()
SEMS = 192
ALL = slice(None)
LOW, HIGH = pl.ds(0, 512), pl.ds(512, 512)
QUERY, KV, OUT = pl.ds(0, 1), pl.ds(1, 2), pl.ds(3, 1)


def tile16(k):
    return pl.ds(pl.multiple_of(k * 16, 16), 16)


def tile128(k):
    return pl.ds(pl.multiple_of(k * 128, 128), 128)


def step_kernel(*refs):
    inputs = Names(("grid", "edge", "count", "edge_w", "enc", "wqkv", "wo", "cot"), refs[:8])
    layer_out, weight_grads = refs[8:10]
    b = Names(tuple(EXCHANGE), refs[10 : 10 + len(EXCHANGE)])
    s = Names(tuple(ATTENTION), refs[10 + len(EXCHANGE) : 10 + len(EXCHANGE) + len(ATTENTION)])
    send_sem, recv_sem, local_sem = refs[10 + len(EXCHANGE) + len(ATTENTION) :]

    member, mp = lax.axis_index("member"), lax.axis_index("mp")
    x, hi, y = lax.div(member, 8), lax.rem(lax.div(member, 4), 2), lax.rem(member, 4)
    g = hi * 16 + mp
    r, grp = lax.rem(mp, 4), lax.div(mp, 4)

    def at_col(place):
        there = lax.rem(place + 32, 32)
        return (x * 8 + lax.div(there, 16) * 4 + y, lax.rem(there, 16))

    def at_x(d):
        return (lax.rem(x + d, 4) * 8 + hi * 4 + y, mp)

    def at_y(d):
        return (x * 8 + hi * 4 + lax.rem(y + d, 4), mp)

    def mate(d):
        return at_col(g - r + lax.rem(r + d, 4))

    started, used, local = [], [0], [0]

    def take(n=1):
        used[0] += n
        return used[0] - n

    def push(src, dst, recv, device):
        copy = pltpu.make_async_remote_copy(
            src_ref=src,
            dst_ref=dst,
            send_sem=send_sem.at[len(started)],
            recv_sem=recv_sem.at[recv],
            device_id=device,
            device_id_type=MESH,
        )
        copy.start()
        started.append(copy)

    def arrived(dst, recv):
        pltpu.make_async_copy(dst, dst, recv_sem.at[recv]).wait()

    def here(src, dst):
        copy = pltpu.make_async_copy(src, dst, local_sem.at[local[0]])
        local[0] += 1
        copy.start()
        return copy

    barrier = pltpu.get_barrier_semaphore()
    sources = [at_col(g + 4 * d) for d in (1, -1, 2, -2)]
    sources += [at_x(d) for d in range(1, 4)] + [at_y(d) for d in range(1, 4)]
    sources += [mate(d) for d in range(1, 4)]
    sources += [at_col(g - r + d) for d in (-2, -1, 4, 5)]
    for device in sources:
        pl.semaphore_signal(barrier, inc=1, device_id=device, device_id_type=MESH)
    own_qkv = here(inputs.wqkv, b.w.at[0, pl.ds(0, 3)])
    own_wo = here(inputs.wo, b.w.at[0, 3])
    edges = [here(getattr(inputs, n), getattr(b, n)) for n in ("edge", "count", "edge_w")]
    own_enc = here(inputs.enc, b.enc)
    own_grid = here(inputs.grid, b.ext.at[pl.ds(GRID_DEV, GRID_DEV)])
    own_cot = here(inputs.cot, b.cot.at[r])
    pl.semaphore_wait(barrier, len(sources))

    piece_a, row_a = (tile16(y), tile128(x)), (tile16(y), LOW)
    piece_b, row_b = (tile16(x), tile128(y + 4)), (tile16(x), HIGH)
    others = pl.ds(1, 3)

    def across(kinds, sems, first, second, at_first, at_second):
        for d in range(1, 4):
            part_a = b.w.at[(others, kinds) + first]
            part_b = b.w.at[(others, kinds) + second]
            push(part_a, part_a, sems + d - 1, at_first(d))
            push(part_b, part_b, sems + 2 + d, at_second(d))

    def across_arrived(kinds, sems, first, second):
        for d in range(3):
            arrived(b.w.at[(others, kinds) + first], sems + d)
            arrived(b.w.at[(others, kinds) + second], sems + 3 + d)

    w_one, w_two = take(12), take(6)
    for n, (j, off_a, off_b) in enumerate(((1, 4, 4), (2, -4, -4), (3, 8, -8))):
        for m, off, piece in ((0, off_a, piece_a), (3, off_b, piece_b)):
            push(inputs.wqkv.at[(ALL,) + piece], b.w.at[(j, pl.ds(0, 3)) + piece], w_one + m + n, at_col(g + off))
            push(inputs.wo.at[piece], b.w.at[(j, 3) + piece], w_one + 6 + m + n, at_col(g + off))

    left_rows, right_rows = pl.ds(0, GRID_DEV), pl.ds(2 * GRID_DEV, GRID_DEV)
    grid_sem = take(2)
    push(inputs.grid, b.ext.at[left_rows], grid_sem, at_col(g + 1))
    push(inputs.grid, b.ext.at[right_rows], grid_sem + 1, at_col(g - 1))

    b.place[...] = jnp.zeros_like(b.place)
    b.ext[pl.ds(3 * GRID_DEV, EXT - 3 * GRID_DEV), :] = jnp.zeros((EXT - 3 * GRID_DEV, 128), BF16)
    for copy in edges:
        copy.wait()
    slot = lax.broadcasted_iota(jnp.int32, (32, 128), 0)
    coef = jnp.where(slot < b.count[...], b.edge_w[...], 0.0)
    index = (b.edge[...] - (mp - 1) * GRID_DEV).astype(F32)
    both = jnp.concatenate([coef, index, jnp.zeros((64, 128), F32)], axis=0).T
    b.coef[...] = both[:, 0:32]
    b.index[...] = both[:, 32:64].astype(jnp.int32)

    def build(k, carry):
        rows = tile16(k)
        start = pl.multiple_of(lax.div(862 + 216 * k, 128) * 128, 128)
        index = b.index[rows, :] - start
        coef = b.coef[rows, :]
        lane = lax.broadcasted_iota(jnp.int32, (16, BAND), 1)
        total = jnp.zeros((16, BAND), F32)
        for e in range(32):
            total += jnp.where(lane == index[:, e : e + 1], coef[:, e : e + 1], 0.0)
        b.place[rows, pl.ds(start, BAND)] = total.astype(BF16)
        return carry

    lax.fori_loop(0, 8, build, 0)

    for n in range(3):
        for m, piece in ((0, piece_a), (3, piece_b)):
            arrived(b.w.at[(n + 1, pl.ds(0, 3)) + piece], w_one + m + n)
            arrived(b.w.at[(n + 1, 3) + piece], w_one + 6 + m + n)
    across(ALL, w_two, piece_a, piece_b, at_x, at_y)
    own_grid.wait()
    arrived(b.ext.at[left_rows], grid_sem)
    arrived(b.ext.at[right_rows], grid_sem + 1)
    node_in = dot(b.place[...], b.ext[...]).astype(BF16)
    b.nodes[pl.ds(r + 2, 1)] = node_in[None]
    mine = b.nodes.at[r + 2]
    mate_sem, next_sem = take(3), take(4)
    near = jnp.where(r < 2, g - r - 4, g - r + 4)
    for d in range(1, 4):
        push(mine, mine, mate_sem + d - 1, mate(d))
    for t in range(4):
        push(mine, b.nodes.at[lax.rem(r + 6, 8)], next_sem + r, at_col(near + t))

    across_arrived(ALL, w_two, piece_a, piece_b)
    w_kv, w_query, w_out = take(6), take(6), take(6)
    for kinds, sems in ((KV, w_kv), (QUERY, w_query), (OUT, w_out)):
        across(kinds, sems, row_a, row_b, at_y, at_x)

    own_cot.wait()
    cot_sem = take(3)
    sibling = r + 1 - 2 * lax.rem(r, 2)
    across = lax.rem(r + 2, 4)
    push(b.cot.at[r], b.cot.at[r], cot_sem, at_col(g - r + across))
    push(b.cot.at[r], b.cot.at[r], cot_sem + 1, at_col(g - r + sibling))

    for d in range(1, 4):
        arrived(mine, mate_sem + d - 1)
    for t, place in enumerate((6, 7, 0, 1)):
        arrived(b.nodes.at[place], next_sem + t)
    own_enc.wait()

    def normalise(k, carry):
        hidden = dot(b.nodes[k], b.enc[...])
        centred = hidden - jnp.mean(hidden, axis=1, keepdims=True)
        spread = jnp.mean(centred * centred, axis=1, keepdims=True)
        b.normed[tile128(k), :] = (centred * lax.rsqrt(spread + 1e-05)).astype(BF16)
        return carry

    lax.fori_loop(0, 8, normalise, 0, unroll=2)

    arrived(b.cot.at[across], cot_sem)
    push(b.cot.at[across], b.cot.at[across], cot_sem + 2, at_col(g - r + sibling))
    own_qkv.wait()
    own_wo.wait()
    across_arrived(KV, w_kv, row_a, row_b)

    sems_1 = [take(6) for _ in range(4)]
    part_sem = take(3)

    def plane_first(c):
        for d in range(1, 4):
            to_y, to_x = lax.rem(y + d, 4), lax.rem(x + d, 4)
            push(b.grads.at[c, :, tile16(to_y), LOW], b.in_a1.at[c, d - 1], sems_1[c] + d - 1, at_y(d))
            push(b.grads.at[c, :, tile16(to_x), HIGH], b.in_b1.at[c, d - 1], sems_1[c] + 2 + d, at_x(d))

    class Unit:
        def __init__(self, first):
            self.kinds = (first, first + 1)
            self.c = pl.ds(first, 2)
            self.two, self.column, self.back, self.rest = take(6), take(7), take(6), take(6)

        def second(self):
            for c in self.kinds:
                for d in range(1, 4):
                    arrived(b.in_a1.at[c, d - 1], sems_1[c] + d - 1)
                    arrived(b.in_b1.at[c, d - 1], sems_1[c] + 2 + d)
                sum_a = b.grads[c, :, tile16(y), LOW].astype(F32)
                sum_b = b.grads[c, :, tile16(x), HIGH].astype(F32)
                for d in range(3):
                    sum_a += b.in_a1[c, d].astype(F32)
                    sum_b += b.in_b1[c, d].astype(F32)
                b.sum_a1[c] = sum_a.astype(BF16)
                b.sum_b1[c] = sum_b.astype(BF16)
            c = self.c
            for d in range(1, 4):
                to_y, to_x = lax.rem(y + d, 4), lax.rem(x + d, 4)
                push(b.sum_a1.at[c, :, :, tile128(to_x)], b.in_a2.at[d - 1, c], self.two + d - 1, at_x(d))
                push(b.sum_b1.at[c, :, :, tile128(to_y)], b.in_b2.at[d - 1, c], self.two + 2 + d, at_y(d))

        def plane_sum(self):
            for d in range(3):
                arrived(b.in_a2.at[d, self.c], self.two + d)
                arrived(b.in_b2.at[d, self.c], self.two + 3 + d)
            for c in self.kinds:
                sum_a = b.sum_a1[c, :, :, tile128(x)].astype(F32)
                sum_b = b.sum_b1[c, :, :, tile128(y)].astype(F32)
                for d in range(3):
                    sum_a += b.in_a2[d, c].astype(F32)
                    sum_b += b.in_b2[d, c].astype(F32)
                b.plane[:, c, 0] = sum_a.astype(BF16)
                b.plane[:, c, 1] = sum_b.astype(BF16)

        def to_all(self):
            self.plane_sum()
            for d in (4, 3, 5, 2, 6, 1, 7):
                push(b.plane.at[SHARD_AT[d], self.c], b.in_z.at[d, self.c], self.column + d - 1, at_col(g + 4 * d))

        def all_sum(self):
            c = self.c
            for d in range(1, 8):
                arrived(b.in_z.at[d, c], self.column + d - 1)
            pairs = [b.plane[0, c].astype(F32) + b.in_z[4, c].astype(F32)]
            pairs += [b.in_z[d, c].astype(F32) + b.in_z[d + 4, c].astype(F32) for d in (1, 2, 3)]
            self.to_plane(((pairs[0] + pairs[2]) + (pairs[1] + pairs[3])).astype(BF16))

        def to_plane(self, total):
            c = self.c
            b.gathered[(c,) + piece_a] = total[:, 0]
            b.gathered[(c,) + piece_b] = total[:, 1]
            for d in range(1, 4):
                part_a, part_b = b.gathered.at[(c,) + piece_a], b.gathered.at[(c,) + piece_b]
                push(part_a, part_a, self.back + d - 1, at_x(d))
                push(part_b, part_b, self.back + 2 + d, at_y(d))

        def to_rest(self):
            c = self.c
            for d in range(3):
                arrived(b.gathered.at[(c,) + piece_a], self.back + d)
                arrived(b.gathered.at[(c,) + piece_b], self.back + 3 + d)
            for d in range(1, 4):
                part_a, part_b = b.gathered.at[(c,) + row_a], b.gathered.at[(c,) + row_b]
                push(part_a, part_a, self.rest + d - 1, at_y(d))
                push(part_b, part_b, self.rest + 2 + d, at_x(d))

        def finish(self):
            c = self.c
            for d in range(3):
                arrived(b.gathered.at[(c,) + row_a], self.rest + d)
                arrived(b.gathered.at[(c,) + row_b], self.rest + 3 + d)
            results.append(here(b.gathered.at[c], weight_grads.at[c]))

    results = []

    def finish(c):
        for d in range(1, 4):
            arrived(b.gathered.at[(c,) + row_a], sems_4[c] + d - 1)
            arrived(b.gathered.at[(c,) + row_b], sems_4[c] + 2 + d)
        results.append(here(b.gathered.at[c], weight_grads.at[c]))

    early, late = Unit(2), Unit(0)

    class Hooks:
        def before_query(self):
            across_arrived(QUERY, w_query, row_a, row_b)

        def before_out(self):
            across_arrived(OUT, w_out, row_a, row_b)
            arrived(b.cot.at[sibling], cot_sem + 1)
            arrived(b.cot.at[lax.rem(sibling + 2, 4)], cot_sem + 2)

        def have_part(self):
            for d in range(1, 4):
                push(b.part.at[lax.rem(r + d, 4)], b.part_in.at[d - 1], part_sem + d - 1, mate(d))

        def have_grad(self, c):
            plane_first(c)

    attention(grp, b.normed, b.w, b.cot, b.grads, b.part, s, Hooks())

    early.second()
    early.to_all()
    late.second()
    out = dot(b.nodes[r + 2], b.enc[...]) + b.part[r].astype(F32)
    for d in range(3):
        arrived(b.part_in.at[d], part_sem + d)
        out += b.part_in[d].astype(F32)
    b.out[...] = out.astype(BF16)
    results.append(here(b.out, layer_out))
    late.to_all()
    early.all_sum()
    early.to_rest()
    late.all_sum()
    early.finish()
    late.to_rest()
    late.finish()
    for copy in results:
        copy.wait()
    for copy in started:
        copy.wait_send()
    assert used[0] <= SEMS and len(started) <= SEMS and local[0] <= 16


def finish_kernel(layer_in, grads, layer_out, grad_qkv, grad_out):
    layer_out[...] = layer_in[...]
    grad_qkv[...] = grads[0:3].astype(F32)
    grad_out[...] = grads[3].astype(F32)


def on_device(
    grid_fields, edge_grid, edge_count, edge_weight, enc_weight, qkv_weight, out_weight, cotangent
):
    vmem, anywhere = pl.BlockSpec(memory_space=pltpu.VMEM), pl.BlockSpec(memory_space=pl.ANY)
    layer_out, grads = pl.pallas_call(
        step_kernel,
        out_shape=(
            jax.ShapeDtypeStruct((128, 1024), BF16),
            jax.ShapeDtypeStruct((4, 64, 1024), BF16),
        ),
        in_specs=[anywhere] * 8,
        out_specs=(anywhere, anywhere),
        scratch_shapes=[
            *EXCHANGE.values(),
            *ATTENTION.values(),
            pltpu.SemaphoreType.DMA((SEMS,)),
            pltpu.SemaphoreType.DMA((SEMS,)),
            pltpu.SemaphoreType.DMA((16,)),
        ],
        compiler_params=pltpu.CompilerParams(
            collective_id=0, has_side_effects=True, vmem_limit_bytes=56 * 1024 * 1024
        ),
    )(
        grid_fields.reshape(GRID_DEV, 128),
        edge_grid.T,
        edge_count.reshape(1, 128),
        edge_weight.T,
        enc_weight,
        qkv_weight,
        out_weight,
        cotangent.reshape(128, 1024),
    )
    layer_out, grad_qkv, grad_out = pl.pallas_call(
        finish_kernel,
        out_shape=(
            jax.ShapeDtypeStruct((128, 1024), BF16),
            jax.ShapeDtypeStruct((3, 64, 1024), F32),
            jax.ShapeDtypeStruct((64, 1024), F32),
        ),
        in_specs=[vmem, vmem],
        out_specs=(vmem, vmem, vmem),
    )(layer_out, grads)
    return layer_out[None], grad_qkv, grad_out


def solution(mesh):
    placed = (
        P("member", "mp", None),
        P("mp", None),
        P("mp"),
        P("mp", None),
        P(),
        P(None, "mp", None),
        P("mp", None),
        P("member", "mp", None),
    )
    return jax.shard_map(
        on_device,
        mesh=mesh,
        in_specs=placed,
        out_specs=(P("member", "mp", None), P(None, "mp", None), P("mp", None)),
        check_vma=False,
    )
```

```python
import functools
import math

import jax
import jax.numpy as jnp
from jax import lax
from jax.experimental import pallas as pl
from jax.experimental.pallas import tpu as pltpu
from jax.sharding import PartitionSpec as P

MESH = pl.DeviceIdType.MESH
BF16, F32 = jnp.bfloat16, jnp.float32
LOG2E = math.log2(math.e)

GRID_DEV = 1728
EXT = 41 * 128
BAND = 17 * 128
KEYS = 768
NT = (((1,), (1,)), ((), ()))
SHARD_AT = {1: 2, 2: 3, 3: 1, 4: 0, 5: 2, 6: 3, 7: 1}


def dot(a, b):
    return jnp.dot(a, b, preferred_element_type=F32)


def dot_nt(a, b):
    return lax.dot_general(a, b, NT, preferred_element_type=F32)


def attention_scratch():
    return dict(
        keys=pltpu.VMEM((1024, 256), BF16),
        keys_t=pltpu.VMEM((256, 1024), BF16),
        values=pltpu.VMEM((1024, 256), BF16),
        values_t=pltpu.VMEM((256, 1024), BF16),
        query=pltpu.VMEM((512, 256), BF16),
        query_tz=pltpu.VMEM((4, 128, 512), BF16),
        d_att_t=pltpu.VMEM((256, 512), BF16),
        bias=pltpu.VMEM((2, KEYS, 256), F32),
        weights=pltpu.VMEM((8, KEYS, 256), BF16),
        row_d=pltpu.VMEM((8, 1, 256), F32),
        d_att_z=pltpu.VMEM((8, 128, 256), BF16),
        att_t=pltpu.VMEM((256, 512), BF16),
        att=pltpu.VMEM((512, 256), BF16),
        d_query_t=pltpu.VMEM((256, 512), BF16),
        d_keys=pltpu.VMEM((1024, 256), F32),
        d_values=pltpu.VMEM((1024, 256), F32),
        left=pltpu.VMEM((256, 1024), BF16),
    )


def weight_grad(grads, c, left, right):
    def tile(t, carry):
        cols = pl.ds(pl.multiple_of(t * 256, 256), 256)
        product = dot(left(), right(cols)).astype(BF16)
        for j in range(4):
            grads[c, j, :, cols] = product[j * 64 : (j + 1) * 64]
        return carry

    lax.fori_loop(0, 4, tile, 0, unroll=True)


def project_attended(w, s, part):
    def project_out(t, carry):
        cols = pl.ds(pl.multiple_of(t * 256, 256), 256)
        product = dot(s.att[...], w[:, 3, :, cols].reshape(256, 256)).astype(BF16)
        for k in range(4):
            part[k, :, cols] = product[k * 128 : (k + 1) * 128]
        return carry

    lax.fori_loop(0, 4, project_out, 0, unroll=True)


def attention(grp, normed, w, cot, grads, part, s, hooks):
    key_pos = lax.broadcasted_iota(jnp.int32, (KEYS, 256), 0)
    query_pos = lax.broadcasted_iota(jnp.int32, (KEYS, 256), 1)
    for qb in range(2):
        node = key_pos + (grp * 512 - 256 + qb * 256)
        inside = (key_pos >= query_pos) & (key_pos <= query_pos + 512) & (node >= 0) & (node < 2048)
        s.bias[qb] = jnp.where(inside, 0.0, -1e30)
    s.d_keys[...] = jnp.zeros_like(s.d_keys)
    s.d_values[...] = jnp.zeros_like(s.d_values)

    wk = w[:, 1].reshape(256, 1024)
    wv = w[:, 2].reshape(256, 1024)

    def project(t, carry):
        rows = pl.ds(pl.multiple_of(t * 256, 256), 256)
        block = normed[rows, :]
        s.keys[rows, :] = dot_nt(block, wk).astype(BF16)
        s.values[rows, :] = dot_nt(block, wv).astype(BF16)
        s.keys_t[:, rows] = dot_nt(wk, block).astype(BF16)
        s.values_t[:, rows] = dot_nt(wv, block).astype(BF16)
        return carry

    lax.fori_loop(0, 4, project, 0, unroll=True)
    hooks.before_query()
    wq = w[:, 0].reshape(256, 1024)

    def project_own(t, carry):
        rows = pl.ds(pl.multiple_of(t * 256, 256), 256)
        block = normed[pl.ds(pl.multiple_of(t * 256 + 256, 256), 256), :]
        s.query[rows, :] = (dot_nt(block, wq) * (LOG2E / 8)).astype(BF16)
        query_t = dot_nt(wq, block) * (LOG2E / 8)
        upper = lax.broadcasted_iota(jnp.int32, (128, 256), 0) < 64
        for h in range(4):
            pair = query_t[h // 2 * 128 : h // 2 * 128 + 128]
            keep = upper if h % 2 == 0 else ~upper
            s.query_tz[h, :, rows] = jnp.where(keep, pair, 0.0).astype(BF16)
        return carry

    lax.fori_loop(0, 2, project_own, 0, unroll=True)
    hooks.before_out()
    wo = w[:, 3].reshape(256, 1024)

    def project_cot(t, carry):
        rows = pl.ds(pl.multiple_of(t * 256, 256), 256)
        cot_rows = cot[pl.ds(t * 2, 2)].reshape(256, 1024)
        s.d_att_t[:, rows] = dot_nt(wo, cot_rows).astype(BF16)
        return carry

    lax.fori_loop(0, 2, project_cot, 0, unroll=True)

    def place(i):
        pair, qb = lax.div(i, 2), lax.rem(i, 2)
        key_rows = pl.ds(pl.multiple_of(qb * 256, 256), KEYS)
        lanes = pl.ds(pl.multiple_of(pair * 128, 128), 128)
        cols = pl.ds(pl.multiple_of(qb * 256, 256), 256)
        return pair, qb, key_rows, lanes, cols

    def head_rows(pair, hh):
        return pl.ds(pl.multiple_of(pair * 128 + hh * 64, 64), 64)

    def forward(i, carry):
        pair, qb, key_rows, lanes, cols = place(i)
        key_block = s.keys[key_rows, lanes]
        scaled, outs = [], []
        scores = [dot(key_block, s.query_tz[pair * 2 + hh, :, cols]) + s.bias[qb] for hh in range(2)]
        tops = [jnp.max(v, axis=0, keepdims=True) for v in scores]
        all_weights, inverses = [], []
        for hh in range(2):
            weight = jnp.exp2(scores[hh] - tops[hh])
            inverses.append(1.0 / jnp.sum(weight, axis=0, keepdims=True))
            all_weights.append(weight.astype(BF16))
            s.weights[i * 2 + hh] = all_weights[hh]
        for hh in range(2):
            rows = head_rows(pair, hh)
            inverse = inverses[hh]
            out = dot(s.values_t[rows, key_rows], all_weights[hh]) * inverse
            d_out = s.d_att_t[rows, cols].astype(F32)
            s.row_d[i * 2 + hh] = jnp.sum(d_out * out, axis=0, keepdims=True) * inverse
            s.att_t[rows, cols] = out.astype(BF16)
            outs.append(out)
            scaled.append(d_out * inverse)
        s.att[cols, lanes] = jnp.concatenate(outs, axis=0).T.astype(BF16)
        both = jnp.concatenate(scaled, axis=0)
        upper = lax.broadcasted_iota(jnp.int32, (128, 256), 0) < 64
        s.d_att_z[i * 2] = jnp.where(upper, both, 0.0).astype(BF16)
        s.d_att_z[i * 2 + 1] = jnp.where(upper, 0.0, both).astype(BF16)
        rows_form = both.T
        low = lax.broadcasted_iota(jnp.int32, (256, 128), 1) < 64
        s.d_values[key_rows, lanes] += dot(
            all_weights[0], jnp.where(low, rows_form, 0.0).astype(BF16)
        ) + dot(all_weights[1], jnp.where(low, 0.0, rows_form).astype(BF16))
        return carry

    lax.fori_loop(0, 4, forward, 0, unroll=True)

    weight_grad(grads, 3, lambda: s.att_t[...], lambda cols: cot[:, :, cols].reshape(512, 256))
    hooks.have_grad(3)
    s.left[...] = s.d_values[...].T.astype(BF16)
    weight_grad(grads, 2, lambda: s.left[...], lambda cols: normed[:, cols])
    hooks.have_grad(2)
    project_attended(w, s, part)
    hooks.have_part()

    def backward(i, carry):
        pair, qb, key_rows, lanes, cols = place(i)
        value_block = s.values[key_rows, lanes]
        low = lax.broadcasted_iota(jnp.int32, (256, 128), 1) < 64
        query = s.query[cols, lanes]
        d_keys = jnp.zeros((KEYS, 128), F32)
        for hh in range(2):
            d_weight = dot(value_block, s.d_att_z[i * 2 + hh])
            d_scores = (s.weights[i * 2 + hh].astype(F32) * (d_weight - s.row_d[i * 2 + hh])).astype(BF16)
            rows = head_rows(pair, hh)
            s.d_query_t[rows, cols] = (dot(s.keys_t[rows, key_rows], d_scores) * 0.125).astype(BF16)
            d_keys += dot(d_scores, jnp.where(low if hh == 0 else ~low, query, jnp.zeros_like(query)))
        s.d_keys[key_rows, lanes] += d_keys * (1.0 / LOG2E)
        return carry

    lax.fori_loop(0, 4, backward, 0, unroll=True)
    weight_grad(grads, 0, lambda: s.d_query_t[...], lambda cols: normed[256:768, cols])
    hooks.have_grad(0)
    s.left[...] = s.d_keys[...].T.astype(BF16)
    weight_grad(grads, 1, lambda: s.left[...], lambda cols: normed[:, cols])
    hooks.have_grad(1)


class Names:
    def __init__(self, names, refs):
        self.__dict__.update(zip(names, refs, strict=True))


def exchange_scratch():
    return dict(
        ext=pltpu.VMEM((EXT, 128), BF16),
        place=pltpu.VMEM((128, EXT), BF16),
        coef=pltpu.VMEM((128, 32), F32),
        nodes=pltpu.VMEM((8, 128, 128), BF16),
        normed=pltpu.VMEM((1024, 1024), BF16),
        w=pltpu.VMEM((4, 4, 64, 1024), BF16),
        cot=pltpu.VMEM((4, 128, 1024), BF16),
        grads=pltpu.VMEM((4, 4, 64, 1024), BF16),
        part=pltpu.VMEM((4, 128, 1024), BF16),
        part_in=pltpu.VMEM((3, 128, 1024), BF16),
        in_a1=pltpu.VMEM((4, 3, 4, 16, 512), BF16),
        in_b1=pltpu.VMEM((4, 3, 4, 16, 512), BF16),
        sum_a1=pltpu.VMEM((4, 4, 16, 512), BF16),
        sum_b1=pltpu.VMEM((4, 4, 16, 512), BF16),
        in_a2=pltpu.VMEM((3, 4, 4, 16, 128), BF16),
        in_b2=pltpu.VMEM((3, 4, 4, 16, 128), BF16),
        plane=pltpu.VMEM((4, 4, 2, 16, 128), BF16),
        in_z=pltpu.VMEM((8, 4, 2, 16, 128), BF16),
        gathered=pltpu.VMEM((4, 64, 1024), BF16),
        out=pltpu.VMEM((128, 1024), BF16),
        edge=pltpu.VMEM((32, 128), jnp.int32),
        count=pltpu.VMEM((1, 128), jnp.int32),
        edge_w=pltpu.VMEM((32, 128), F32),
        enc=pltpu.VMEM((128, 1024), BF16),
        index=pltpu.VMEM((128, 32), jnp.int32),
    )


EXCHANGE = exchange_scratch()
ATTENTION = attention_scratch()
SEMS = 192
ALL = slice(None)
LOW, HIGH = pl.ds(0, 512), pl.ds(512, 512)
QUERY, KV, OUT = pl.ds(0, 1), pl.ds(1, 2), pl.ds(3, 1)


def tile16(k):
    return pl.ds(pl.multiple_of(k * 16, 16), 16)


def tile128(k):
    return pl.ds(pl.multiple_of(k * 128, 128), 128)


def step_kernel(*refs):
    inputs = Names(("grid", "edge", "count", "edge_w", "enc", "wqkv", "wo", "cot"), refs[:8])
    layer_out, weight_grads = refs[8:10]
    b = Names(tuple(EXCHANGE), refs[10 : 10 + len(EXCHANGE)])
    s = Names(tuple(ATTENTION), refs[10 + len(EXCHANGE) : 10 + len(EXCHANGE) + len(ATTENTION)])
    send_sem, recv_sem, local_sem = refs[10 + len(EXCHANGE) + len(ATTENTION) :]

    member, mp = lax.axis_index("member"), lax.axis_index("mp")
    x, hi, y = lax.div(member, 8), lax.rem(lax.div(member, 4), 2), lax.rem(member, 4)
    g = hi * 16 + mp
    r, grp = lax.rem(mp, 4), lax.div(mp, 4)

    def at_col(place):
        there = lax.rem(place + 32, 32)
        return (x * 8 + lax.div(there, 16) * 4 + y, lax.rem(there, 16))

    def at_x(d):
        return (lax.rem(x + d, 4) * 8 + hi * 4 + y, mp)

    def at_y(d):
        return (x * 8 + hi * 4 + lax.rem(y + d, 4), mp)

    def mate(d):
        return at_col(g - r + lax.rem(r + d, 4))

    started, used, local = [], [0], [0]

    def take(n=1):
        used[0] += n
        return used[0] - n

    def push(src, dst, recv, device):
        copy = pltpu.make_async_remote_copy(
            src_ref=src,
            dst_ref=dst,
            send_sem=send_sem.at[len(started)],
            recv_sem=recv_sem.at[recv],
            device_id=device,
            device_id_type=MESH,
        )
        copy.start()
        started.append(copy)

    def arrived(dst, recv):
        pltpu.make_async_copy(dst, dst, recv_sem.at[recv]).wait()

    def here(src, dst):
        copy = pltpu.make_async_copy(src, dst, local_sem.at[local[0]])
        local[0] += 1
        copy.start()
        return copy

    barrier = pltpu.get_barrier_semaphore()
    sources = [at_col(g + 4 * d) for d in (1, -1, 2, -2)]
    sources += [at_x(d) for d in range(1, 4)] + [at_y(d) for d in range(1, 4)]
    sources += [mate(d) for d in range(1, 4)]
    sources += [at_col(g - r + d) for d in (-2, -1, 4, 5)]
    for device in sources:
        pl.semaphore_signal(barrier, inc=1, device_id=device, device_id_type=MESH)
    own_qkv = here(inputs.wqkv, b.w.at[0, pl.ds(0, 3)])
    own_wo = here(inputs.wo, b.w.at[0, 3])
    edges = [here(getattr(inputs, n), getattr(b, n)) for n in ("edge", "count", "edge_w")]
    own_enc = here(inputs.enc, b.enc)
    own_grid = here(inputs.grid, b.ext.at[pl.ds(GRID_DEV, GRID_DEV)])
    own_cot = here(inputs.cot, b.cot.at[r])
    pl.semaphore_wait(barrier, len(sources))

    piece_a, row_a = (tile16(y), tile128(x)), (tile16(y), LOW)
    piece_b, row_b = (tile16(x), tile128(y + 4)), (tile16(x), HIGH)
    others = pl.ds(1, 3)

    def across(kinds, sems, first, second, at_first, at_second):
        for d in range(1, 4):
            part_a = b.w.at[(others, kinds) + first]
            part_b = b.w.at[(others, kinds) + second]
            push(part_a, part_a, sems + d - 1, at_first(d))
            push(part_b, part_b, sems + 2 + d, at_second(d))

    def across_arrived(kinds, sems, first, second):
        for d in range(3):
            arrived(b.w.at[(others, kinds) + first], sems + d)
            arrived(b.w.at[(others, kinds) + second], sems + 3 + d)

    w_one, w_two = take(12), take(6)
    for n, (j, off_a, off_b) in enumerate(((1, 4, 4), (2, -4, -4), (3, 8, -8))):
        for m, off, piece in ((0, off_a, piece_a), (3, off_b, piece_b)):
            push(inputs.wqkv.at[(ALL,) + piece], b.w.at[(j, pl.ds(0, 3)) + piece], w_one + m + n, at_col(g + off))
            push(inputs.wo.at[piece], b.w.at[(j, 3) + piece], w_one + 6 + m + n, at_col(g + off))

    left_rows, right_rows = pl.ds(0, GRID_DEV), pl.ds(2 * GRID_DEV, GRID_DEV)
    grid_sem = take(2)
    push(inputs.grid, b.ext.at[left_rows], grid_sem, at_col(g + 1))
    push(inputs.grid, b.ext.at[right_rows], grid_sem + 1, at_col(g - 1))

    b.place[...] = jnp.zeros_like(b.place)
    b.ext[pl.ds(3 * GRID_DEV, EXT - 3 * GRID_DEV), :] = jnp.zeros((EXT - 3 * GRID_DEV, 128), BF16)
    for copy in edges:
        copy.wait()
    slot = lax.broadcasted_iota(jnp.int32, (32, 128), 0)
    coef = jnp.where(slot < b.count[...], b.edge_w[...], 0.0)
    index = (b.edge[...] - (mp - 1) * GRID_DEV).astype(F32)
    both = jnp.concatenate([coef, index, jnp.zeros((64, 128), F32)], axis=0).T
    b.coef[...] = both[:, 0:32]
    b.index[...] = both[:, 32:64].astype(jnp.int32)

    def build(k, carry):
        rows = tile16(k)
        start = pl.multiple_of(lax.div(862 + 216 * k, 128) * 128, 128)
        index = b.index[rows, :] - start
        coef = b.coef[rows, :]
        lane = lax.broadcasted_iota(jnp.int32, (16, BAND), 1)
        total = jnp.zeros((16, BAND), F32)
        for e in range(32):
            total += jnp.where(lane == index[:, e : e + 1], coef[:, e : e + 1], 0.0)
        b.place[rows, pl.ds(start, BAND)] = total.astype(BF16)
        return carry

    lax.fori_loop(0, 8, build, 0)

    for n in range(3):
        for m, piece in ((0, piece_a), (3, piece_b)):
            arrived(b.w.at[(n + 1, pl.ds(0, 3)) + piece], w_one + m + n)
            arrived(b.w.at[(n + 1, 3) + piece], w_one + 6 + m + n)
    across(ALL, w_two, piece_a, piece_b, at_x, at_y)
    own_grid.wait()
    arrived(b.ext.at[left_rows], grid_sem)
    arrived(b.ext.at[right_rows], grid_sem + 1)
    node_in = dot(b.place[...], b.ext[...]).astype(BF16)
    b.nodes[pl.ds(r + 2, 1)] = node_in[None]
    mine = b.nodes.at[r + 2]
    mate_sem, next_sem = take(3), take(4)
    near = jnp.where(r < 2, g - r - 4, g - r + 4)
    for d in range(1, 4):
        push(mine, mine, mate_sem + d - 1, mate(d))
    for t in range(4):
        push(mine, b.nodes.at[lax.rem(r + 6, 8)], next_sem + r, at_col(near + t))

    across_arrived(ALL, w_two, piece_a, piece_b)
    w_kv, w_query, w_out = take(6), take(6), take(6)
    for kinds, sems in ((KV, w_kv), (QUERY, w_query), (OUT, w_out)):
        across(kinds, sems, row_a, row_b, at_y, at_x)

    own_cot.wait()
    cot_sem = take(3)
    sibling = r + 1 - 2 * lax.rem(r, 2)
    across = lax.rem(r + 2, 4)
    push(b.cot.at[r], b.cot.at[r], cot_sem, at_col(g - r + across))
    push(b.cot.at[r], b.cot.at[r], cot_sem + 1, at_col(g - r + sibling))

    for d in range(1, 4):
        arrived(mine, mate_sem + d - 1)
    for t, place in enumerate((6, 7, 0, 1)):
        arrived(b.nodes.at[place], next_sem + t)
    own_enc.wait()

    def normalise(k, carry):
        hidden = dot(b.nodes[k], b.enc[...])
        centred = hidden - jnp.mean(hidden, axis=1, keepdims=True)
        spread = jnp.mean(centred * centred, axis=1, keepdims=True)
        b.normed[tile128(k), :] = (centred * lax.rsqrt(spread + 1e-05)).astype(BF16)
        return carry

    lax.fori_loop(0, 8, normalise, 0, unroll=2)

    arrived(b.cot.at[across], cot_sem)
    push(b.cot.at[across], b.cot.at[across], cot_sem + 2, at_col(g - r + sibling))
    own_qkv.wait()
    own_wo.wait()
    across_arrived(KV, w_kv, row_a, row_b)

    sems_1 = [take(6) for _ in range(4)]
    part_sem = take(3)

    def plane_first(c):
        for d in range(1, 4):
            to_y, to_x = lax.rem(y + d, 4), lax.rem(x + d, 4)
            push(b.grads.at[c, :, tile16(to_y), LOW], b.in_a1.at[c, d - 1], sems_1[c] + d - 1, at_y(d))
            push(b.grads.at[c, :, tile16(to_x), HIGH], b.in_b1.at[c, d - 1], sems_1[c] + 2 + d, at_x(d))

    class Unit:
        def __init__(self, first):
            self.kinds = (first, first + 1)
            self.c = pl.ds(first, 2)
            self.two, self.column, self.back, self.rest = take(6), take(7), take(6), take(6)

        def second(self):
            for c in self.kinds:
                for d in range(1, 4):
                    arrived(b.in_a1.at[c, d - 1], sems_1[c] + d - 1)
                    arrived(b.in_b1.at[c, d - 1], sems_1[c] + 2 + d)
                sum_a = b.grads[c, :, tile16(y), LOW].astype(F32)
                sum_b = b.grads[c, :, tile16(x), HIGH].astype(F32)
                for d in range(3):
                    sum_a += b.in_a1[c, d].astype(F32)
                    sum_b += b.in_b1[c, d].astype(F32)
                b.sum_a1[c] = sum_a.astype(BF16)
                b.sum_b1[c] = sum_b.astype(BF16)
            c = self.c
            for d in range(1, 4):
                to_y, to_x = lax.rem(y + d, 4), lax.rem(x + d, 4)
                push(b.sum_a1.at[c, :, :, tile128(to_x)], b.in_a2.at[d - 1, c], self.two + d - 1, at_x(d))
                push(b.sum_b1.at[c, :, :, tile128(to_y)], b.in_b2.at[d - 1, c], self.two + 2 + d, at_y(d))

        def plane_sum(self):
            for d in range(3):
                arrived(b.in_a2.at[d, self.c], self.two + d)
                arrived(b.in_b2.at[d, self.c], self.two + 3 + d)
            for c in self.kinds:
                sum_a = b.sum_a1[c, :, :, tile128(x)].astype(F32)
                sum_b = b.sum_b1[c, :, :, tile128(y)].astype(F32)
                for d in range(3):
                    sum_a += b.in_a2[d, c].astype(F32)
                    sum_b += b.in_b2[d, c].astype(F32)
                b.plane[:, c, 0] = sum_a.astype(BF16)
                b.plane[:, c, 1] = sum_b.astype(BF16)

        def to_all(self):
            self.plane_sum()
            for d in (4, 3, 5, 2, 6, 1, 7):
                push(b.plane.at[SHARD_AT[d], self.c], b.in_z.at[d, self.c], self.column + d - 1, at_col(g + 4 * d))

        def all_sum(self):
            c = self.c
            for d in range(1, 8):
                arrived(b.in_z.at[d, c], self.column + d - 1)
            pairs = [b.plane[0, c].astype(F32) + b.in_z[4, c].astype(F32)]
            pairs += [b.in_z[d, c].astype(F32) + b.in_z[d + 4, c].astype(F32) for d in (1, 2, 3)]
            self.to_plane(((pairs[0] + pairs[2]) + (pairs[1] + pairs[3])).astype(BF16))

        def to_plane(self, total):
            c = self.c
            b.gathered[(c,) + piece_a] = total[:, 0]
            b.gathered[(c,) + piece_b] = total[:, 1]
            for d in range(1, 4):
                part_a, part_b = b.gathered.at[(c,) + piece_a], b.gathered.at[(c,) + piece_b]
                push(part_a, part_a, self.back + d - 1, at_x(d))
                push(part_b, part_b, self.back + 2 + d, at_y(d))

        def to_rest(self):
            c = self.c
            for d in range(3):
                arrived(b.gathered.at[(c,) + piece_a], self.back + d)
                arrived(b.gathered.at[(c,) + piece_b], self.back + 3 + d)
            for d in range(1, 4):
                part_a, part_b = b.gathered.at[(c,) + row_a], b.gathered.at[(c,) + row_b]
                push(part_a, part_a, self.rest + d - 1, at_y(d))
                push(part_b, part_b, self.rest + 2 + d, at_x(d))

        def finish(self):
            c = self.c
            for d in range(3):
                arrived(b.gathered.at[(c,) + row_a], self.rest + d)
                arrived(b.gathered.at[(c,) + row_b], self.rest + 3 + d)
            results.append(here(b.gathered.at[c], weight_grads.at[c]))

    results = []

    def finish(c):
        for d in range(1, 4):
            arrived(b.gathered.at[(c,) + row_a], sems_4[c] + d - 1)
            arrived(b.gathered.at[(c,) + row_b], sems_4[c] + 2 + d)
        results.append(here(b.gathered.at[c], weight_grads.at[c]))

    early, late = Unit(2), Unit(0)

    class Hooks:
        def before_query(self):
            across_arrived(QUERY, w_query, row_a, row_b)

        def before_out(self):
            across_arrived(OUT, w_out, row_a, row_b)
            arrived(b.cot.at[sibling], cot_sem + 1)
            arrived(b.cot.at[lax.rem(sibling + 2, 4)], cot_sem + 2)

        def have_part(self):
            for d in range(1, 4):
                push(b.part.at[lax.rem(r + d, 4)], b.part_in.at[d - 1], part_sem + d - 1, mate(d))

        def have_grad(self, c):
            plane_first(c)

    attention(grp, b.normed, b.w, b.cot, b.grads, b.part, s, Hooks())

    early.second()
    early.to_all()
    late.second()
    out = dot(b.nodes[r + 2], b.enc[...]) + b.part[r].astype(F32)
    for d in range(3):
        arrived(b.part_in.at[d], part_sem + d)
        out += b.part_in[d].astype(F32)
    b.out[...] = out.astype(BF16)
    results.append(here(b.out, layer_out))
    late.to_all()
    early.all_sum()
    early.to_rest()
    late.all_sum()
    early.finish()
    late.to_rest()
    late.finish()
    for copy in results:
        copy.wait()
    for copy in started:
        copy.wait_send()
    assert used[0] <= SEMS and len(started) <= SEMS and local[0] <= 16


def finish_kernel(layer_in, grads, layer_out, grad_qkv, grad_out, narrow, wide, in_sem, out_sem):
    layer = pltpu.make_async_copy(layer_in, layer_out, in_sem.at[4])
    reads = [pltpu.make_async_copy(grads.at[c], narrow.at[c], in_sem.at[c]) for c in range(4)]
    for copy in (*reads, layer):
        copy.start()
    writes = []
    for c in range(4):
        reads[c].wait()
        wide[c] = narrow[c].astype(F32)
        writes.append(pltpu.make_async_copy(wide.at[c], grad_qkv.at[c] if c < 3 else grad_out, out_sem.at[c]))
        writes[c].start()
    for copy in (*writes, layer):
        copy.wait()


def on_device(
    grid_fields, edge_grid, edge_count, edge_weight, enc_weight, qkv_weight, out_weight, cotangent
):
    anywhere = pl.BlockSpec(memory_space=pl.ANY)
    layer_out, grads = pl.pallas_call(
        step_kernel,
        out_shape=(
            jax.ShapeDtypeStruct((128, 1024), BF16),
            jax.ShapeDtypeStruct((4, 64, 1024), BF16),
        ),
        in_specs=[anywhere] * 8,
        out_specs=(anywhere, anywhere),
        scratch_shapes=[
            *EXCHANGE.values(),
            *ATTENTION.values(),
            pltpu.SemaphoreType.DMA((SEMS,)),
            pltpu.SemaphoreType.DMA((SEMS,)),
            pltpu.SemaphoreType.DMA((16,)),
        ],
        compiler_params=pltpu.CompilerParams(
            collective_id=0, has_side_effects=True, vmem_limit_bytes=56 * 1024 * 1024
        ),
    )(
        grid_fields.reshape(GRID_DEV, 128),
        edge_grid.T,
        edge_count.reshape(1, 128),
        edge_weight.T,
        enc_weight,
        qkv_weight,
        out_weight,
        cotangent.reshape(128, 1024),
    )
    layer_out, grad_qkv, grad_out = pl.pallas_call(
        finish_kernel,
        out_shape=(
            jax.ShapeDtypeStruct((128, 1024), BF16),
            jax.ShapeDtypeStruct((3, 64, 1024), F32),
            jax.ShapeDtypeStruct((64, 1024), F32),
        ),
        in_specs=[anywhere] * 2,
        out_specs=(anywhere,) * 3,
        scratch_shapes=[
            pltpu.VMEM((4, 64, 1024), BF16),
            pltpu.VMEM((4, 64, 1024), F32),
            pltpu.SemaphoreType.DMA((5,)),
            pltpu.SemaphoreType.DMA((4,)),
        ],
    )(layer_out, grads)
    return layer_out[None], grad_qkv, grad_out


def solution(mesh):
    placed = (
        P("member", "mp", None),
        P("mp", None),
        P("mp"),
        P("mp", None),
        P(),
        P(None, "mp", None),
        P("mp", None),
        P("member", "mp", None),
    )
    return jax.shard_map(
        on_device,
        mesh=mesh,
        in_specs=placed,
        out_specs=(P("member", "mp", None), P(None, "mp", None), P("mp", None)),
        check_vma=False,
    )
```
